128 devices in a mesh: dp: 16 (over z, x_hi, core), tensor: 8 (over y, x_lo).
Axes of the slice: x: 4 (x_hi: 2, x_lo: 2; x = x_hi * 2 + x_lo), y: 4, z: 4, core: 2. Of those that a mesh axis runs over, the one named last changes fastest.
Arguments:
- query_states: bfloat16 [16, 512, 8192], P('dp', None, 'tensor'), may hold values from -110 to 110
- key_states: bfloat16 [16, 512, 1024], P('dp', None, 'tensor'), may hold values from -4 to 4
- value_states: bfloat16 [16, 512, 1024], P('dp', None, 'tensor'), may hold values from -6 to 6
- segment_ids: int32 [16, 512], P('dp', 'tensor'), may hold values from 0 to 7, never falling along the last dimension, each value on 1 to 256 neighbouring positions
- pair_margins: float32 [16, 4], P('dp'), may hold values from -6 to 6
- upstream: bfloat16 [16, 512, 8192], P('dp', 'tensor'), may hold values from -6 to 6
- out_weight: bfloat16 [8192, 8192], P('tensor', 'dp'), may hold values from -0.0625 to 0.0625
Outputs:
- query_grad: bfloat16 [16, 512, 8192], P('dp', None, 'tensor')
- key_grad: bfloat16 [16, 512, 1024], P('dp', None, 'tensor')
- value_grad: bfloat16 [16, 512, 1024], P('dp', None, 'tensor')
- out_weight_grad: float32 [8192, 8192], P('tensor', 'dp')
The draws below stay inside these ranges and needn't reach their ends.
Inputs may be any that keep to these rules, and one draw needn't show every extreme that they name: `segment_ids`: every row holds all 8 responses, each of 1 to 256 positions in order.
All inputs are finite; a program needn't handle non-finite values.
Results may differ from the reference program's by a relative error of at most 0.015.
Values may be sent and summed in bfloat16 or wider, within the bound.
No kernel may reach another device: no remote copies, remote signals or barrier semaphores. Data moves between devices by JAX's collectives and lax.ppermute only.
A program may use at most 128 MiB of HBM per device.

```python
import math
import jax
import jax.numpy as jnp
import numpy as np
from jax import lax

D = 8192
HEADS = 64
KV_HEADS = 8
HD = 128
R_DEV = 1
SEGS = 8
SEG_MOST = 256
ROW_LEN = 512
ROWS = 16
PAIRS = 4


def base_keys(key):
    drawn = jax.random.normal(jax.random.fold_in(key, 11), (ROWS, ROW_LEN, KV_HEADS * HD), jnp.float32)
    return jnp.clip(drawn, -4.0, 4.0)


def draw_key_states(key, part):
    keys_drawn = base_keys(key)
    return keys_drawn.astype(jnp.bfloat16)


def draw_query_states(key, part):
    drawn = jax.random.normal(jax.random.fold_in(key, 13), (ROWS, ROW_LEN, HEADS * HD), jnp.float32)
    drawn = jnp.clip(drawn, -4.0, 4.0)
    return drawn.astype(jnp.bfloat16)


def spiked(result, own_key, source, target, parts, factor):
    def block_of(dim):
        return (jnp.arange(result.shape[dim]) // (result.shape[dim] // parts)).reshape((-1,) + (1,) * (result.ndim - 1 - dim))

    one_side = jax.random.permutation(own_key, parts)[block_of(target)]
    far = (block_of(target) + parts // 2) % parts
    return jnp.where((block_of(source) == one_side) | (block_of(source) == far), factor * result, result)


def shard_levels(rng, shape, split, least, high):
    def one(axis_at, blocks):
        steps = jax.random.uniform(jax.random.fold_in(jax.random.fold_in(rng, 6), axis_at), (blocks,), jnp.float32, least / len(split), high / len(split))
        return jnp.repeat(jnp.exp(steps), shape[axis_at] // blocks).reshape((-1,) + (1,) * (len(shape) - axis_at - 1))

    gain = one(*split[0])
    for cut in split[1:]:
        gain = gain * one(*cut)
    return gain


def length_profile(number_of, total, most, slope):
    weights = [(1 << 20) // math.isqrt(grade ** slope) + 1 for grade in range(2, number_of + 1)]
    spare, holding = total - most - (number_of - 1), [1] * (number_of - 1)
    while spare > 0:
        movable = [i for i in range(number_of - 1) if holding[i] < most]
        mass, remaining = sum([weights[i] for i in movable]), spare
        for i in movable:
            more = min(most - holding[i], max(1, remaining * weights[i] // mass), spare)
            holding[i] = holding[i] + more
            spare = spare - more
    return np.array([most] + holding)


def uneven_parts(own_key, number_of, total, reach, skew):
    if number_of == 2:
        one = jax.random.randint(own_key, (), max(1, total - reach), min(reach, total - 1) + 1)
        return jnp.stack([one, total - one])
    lengths = jnp.asarray(length_profile(number_of, total, reach, skew), jnp.int32)
    couples = (number_of - 1) // 2
    giver, receiver = lengths[1:1 + 2 * couples:2], lengths[2:2 + 2 * couples:2]
    margin = jnp.minimum(giver - 1, reach - receiver)
    passed = jax.random.randint(jax.random.fold_in(own_key, 1), (couples,), 0, 1 << 20) % (margin + 1)
    lengths = lengths.at[1:1 + 2 * couples:2].set(giver - passed).at[2:2 + 2 * couples:2].set(receiver + passed)
    return lengths[jax.random.permutation(jax.random.fold_in(own_key, 2), number_of)]


def scatter_about(key, shape, scale, bound, cuts=(), kind=jnp.bfloat16):
    factor_of = shard_levels(key, shape, cuts, -0.22, 0.18) if cuts else 1.0
    result = jax.random.normal(key, shape, jnp.float32) * scale * factor_of
    return jnp.minimum(jnp.maximum(result, -bound), bound).astype(kind)


def gaussian_with(rng, shape, deviation, reach, shards, heavy, held_as=jnp.bfloat16):
    values = deviation * jax.random.normal(rng, shape, jnp.float32)
    if shards:
        values = values * shard_levels(rng, shape, shards, -0.22, 0.18)
    return jnp.clip(spiked(values, jax.random.fold_in(rng, 3), *heavy), -reach, reach).astype(held_as)


def setup_inputs(seed: int = 0) -> dict:
    key_list = jax.random.split(jax.random.key(seed), 8)
    return {
        "query_states": draw_query_states(jax.random.fold_in(key_list[7], 71), 0),
        "key_states": draw_key_states(jax.random.fold_in(key_list[7], 71), 0),
        "value_states": scatter_about(key_list[2], (ROWS, ROW_LEN, KV_HEADS * HD), 1.0, 6.0, ((0, 16), (2, 8))),
        "segment_ids": jax.vmap(lambda own: jnp.searchsorted(jnp.cumsum(uneven_parts(own, SEGS, ROW_LEN, SEG_MOST, 2)), jnp.arange(ROW_LEN), side="right"))(jax.random.split(key_list[3], ROWS)).reshape((ROWS, ROW_LEN)).astype(jnp.int32),
        "pair_margins": scatter_about(key_list[4], (ROWS, PAIRS), 2.0, 6.0, ((0, 16),), jnp.float32),
        "upstream": gaussian_with(key_list[5], (ROWS, ROW_LEN, D), 1.0, 6.0, ((0, 16), (1, 8)), (0, 2, 16, 2.0)),
        "out_weight": scatter_about(key_list[6], (HEADS * HD, D), (HEADS * HD) ** -0.5, 0.0625, ((0, 8), (1, 16))),
    }


def row_terms(inputs, out_weight):
    queries, keys, values, segs, margins, upstream = inputs
    length = queries.shape[0]
    group_size = HEADS // KV_HEADS
    score_scale = HD ** -0.5
    query_heads = queries.astype(jnp.float32).reshape(length, KV_HEADS, group_size, HD)
    key_heads = keys.astype(jnp.float32).reshape(length, KV_HEADS, HD)
    value_heads = values.astype(jnp.float32).reshape(length, KV_HEADS, HD)
    sigma = jax.nn.sigmoid(-margins)
    onehot = (segs[:, None] // 2 == jnp.arange(PAIRS, dtype=jnp.int32)[None, :]).astype(jnp.float32)
    coeff = jnp.sum(onehot * sigma[None, :], axis=1)
    signs = jnp.where(segs % 2 == 0, -1.0, 1.0).astype(jnp.float32)
    output_grad = (upstream.astype(jnp.float32) * (signs * coeff)[:, None]).astype(jnp.bfloat16)
    position = jnp.arange(length, dtype=jnp.int32)
    allowed = (segs[:, None] == segs[None, :]) & (position[None, :] <= position[:, None])
    scores = jnp.einsum("igmd,jgd->gmij", query_heads, key_heads) * score_scale
    scores = jnp.where(allowed[None, None], scores, -1e30)
    highest = jnp.max(scores, axis=-1, keepdims=True)
    expo = jnp.exp(scores - highest)
    probs = expo / jnp.sum(expo, axis=-1, keepdims=True)
    probs_low = lax.optimization_barrier(probs.astype(jnp.bfloat16)).astype(jnp.float32)
    attn_out = jnp.einsum("gmij,jgd->igmd", probs_low, value_heads).astype(jnp.bfloat16).reshape(length, HEADS * HD)
    attn_grad = jnp.dot(output_grad, out_weight.T, preferred_element_type=jnp.float32).astype(jnp.bfloat16)
    row_wgrad = jnp.dot(attn_out.T, output_grad, preferred_element_type=jnp.float32)
    grad_heads = lax.optimization_barrier(attn_grad).astype(jnp.float32).reshape(length, KV_HEADS, group_size, HD)
    prob_grad = jnp.einsum("igmd,jgd->gmij", grad_heads, value_heads)
    delta = jnp.sum(probs * prob_grad, axis=-1, keepdims=True)
    score_grad = lax.optimization_barrier((score_scale * probs * (prob_grad - delta)).astype(jnp.bfloat16)).astype(jnp.float32)
    query_grad = jnp.einsum("gmij,jgd->igmd", score_grad, key_heads).astype(jnp.bfloat16).reshape(length, HEADS * HD)
    key_grad = jnp.einsum("gmij,igmd->jgd", score_grad, query_heads).astype(jnp.bfloat16).reshape(length, KV_HEADS * HD)
    value_grad = jnp.einsum("gmij,igmd->jgd", probs_low, grad_heads).astype(jnp.bfloat16).reshape(length, KV_HEADS * HD)
    return row_wgrad, (query_grad, key_grad, value_grad)


def reference(query_states, key_states, value_states, segment_ids, pair_margins, upstream, out_weight):
    start_sum = jnp.zeros((HEADS * HD, D), jnp.float32)
    start_group = jnp.zeros((HEADS * HD, D), jnp.float32)
    row_index = jnp.arange(ROWS, dtype=jnp.int32)

    def step_fn(carry, inputs):
        total, group_acc = carry
        index = inputs[0]
        row_wgrad, grads = row_terms(inputs[1:], out_weight)
        group_acc = group_acc + row_wgrad
        closing = (index + 1) % R_DEV == 0
        rounded = lax.optimization_barrier(group_acc.astype(jnp.bfloat16)).astype(jnp.float32)
        total = jnp.where(closing, total + rounded, total)
        group_acc = jnp.where(closing, jnp.zeros_like(group_acc), group_acc)
        return (total, group_acc), grads

    carry, grads = lax.scan(step_fn, (start_sum, start_group), (row_index, query_states, key_states, value_states, segment_ids, pair_margins, upstream))
    return grads[0], grads[1], grads[2], carry[0]
```

```python
import jax
import jax.numpy as jnp
from jax import lax
from jax.sharding import PartitionSpec as P

HD = 128
F32 = jnp.float32
BF16 = jnp.bfloat16


def by_dp(step):
    return [(i, step(i)) for i in range(16)]


def by_tensor(step):
    return [(i, step(i)) for i in range(8)]


SIBLING = by_dp(lambda i: i ^ 1)
ACROSS = by_dp(lambda i: i ^ 2)
Z_UP = by_dp(lambda i: (i + 4) % 16)
Z_DOWN = by_dp(lambda i: (i - 4) % 16)
PAIR = by_tensor(lambda i: i ^ 1)
Y_UP = by_tensor(lambda i: (i + 2) % 8)
Y_DOWN = by_tensor(lambda i: (i - 2) % 8)


def sibling(x):
    return lax.ppermute(x, "dp", SIBLING)


def across(x):
    return lax.ppermute(x, "dp", ACROSS)


def z_up(x):
    return lax.ppermute(x, "dp", Z_UP)


def z_down(x):
    return lax.ppermute(x, "dp", Z_DOWN)


def pair(x):
    return lax.ppermute(x, "tensor", PAIR)


def y_up(x):
    return lax.ppermute(x, "tensor", Y_UP)


def y_down(x):
    return lax.ppermute(x, "tensor", Y_DOWN)


def y_gather(x, up_twice):
    behind = y_up(x)
    ahead = y_down(x)
    far = y_up(behind) if up_twice else y_down(ahead)
    return [x, ahead, far, behind]


def pick(x, index, axis):
    return lax.dynamic_index_in_dim(x, index, axis, keepdims=False)


def nt(a, b):
    return lax.dot_general(a, b, (((1,), (1,)), ((), ())), preferred_element_type=F32)


def tn(a, b):
    return lax.dot_general(a, b, (((0,), (0,)), ((), ())), preferred_element_type=F32)


def shards(query_states, key_states, value_states, segment_ids, pair_margins, upstream, out_weight):
    length = query_states.shape[1]
    heads = query_states.shape[2] // HD
    seq = upstream.shape[1]
    score_scale = HD ** (-0.5)
    d = lax.axis_index("dp")
    t = lax.axis_index("tensor")
    z, h, c = d // 4, (d // 2) % 2, d % 2
    y, low = t // 2, t % 2

    sigma = jax.nn.sigmoid(-pair_margins[0])
    segs = segment_ids[0]
    onehot = (segs[:, None] // 2 == jnp.arange(sigma.shape[0], dtype=jnp.int32)[None, :]).astype(F32)
    coeff = jnp.sum(onehot * sigma[None, :], axis=1)
    factor = coeff * jnp.where(segs % 2 == 0, -1.0, 1.0).astype(F32)
    width = upstream.shape[2] // 16
    up = upstream[0].reshape(seq, 4, 2, 2, width)

    def columns(hh, cc):
        parts = [
            lax.dynamic_slice(up, (0, (z + k) % 4, hh, cc, 0), (seq, 1, 1, 1, width)).reshape(seq, width)
            for k in range(4)
        ]
        x = jnp.concatenate(parts, axis=1)
        return (x.astype(F32) * factor[:, None]).astype(BF16)

    own = columns(h, c)
    to_sibling = columns(h, 1 - c)
    to_across = jnp.stack([columns(1 - h, c), columns(1 - h, 1 - c)])
    from_across = across(to_across)
    from_sibling = sibling(to_sibling)
    near = jnp.stack([own, from_sibling])
    other = jnp.stack([from_across[0], sibling(from_across[1])])

    whole_segs = lax.all_gather(segment_ids, "tensor", axis=0, tiled=False).reshape(length)

    half = out_weight.shape[0] // 2
    w_behind = z_up(out_weight)
    w_ahead = z_down(out_weight)
    w_far = jnp.concatenate([z_up(w_behind[:half]), z_down(w_ahead[half:])], axis=0)
    weight = jnp.concatenate([out_weight, w_ahead, w_far, w_behind], axis=1)

    near_pair = pair(near)
    other_pair = pair(other)
    blocks = [
        y_gather(near, True),
        y_gather(other, False),
        y_gather(other_pair, True),
        y_gather(near_pair, False),
    ]
    blocks = [jnp.stack(b).reshape(4 * 2 * seq, 4 * width) for b in blocks]

    query_heads = query_states.reshape(length, heads, HD)
    key_head = key_states[0]
    value_head = value_states[0]
    position = jnp.arange(length, dtype=jnp.int32)
    allowed = (whole_segs[:, None] == whole_segs[None, :]) & (position[None, :] <= position[:, None])
    scores = jnp.einsum("imd,jd->mij", query_heads, key_head, preferred_element_type=F32) * score_scale
    scores = jnp.where(allowed[None], scores, -1e30)
    highest = jnp.max(scores, axis=-1, keepdims=True)
    expo = jnp.exp(scores - highest)
    probs = expo / jnp.sum(expo, axis=-1, keepdims=True)
    probs_low = probs.astype(BF16)
    attn_out = jnp.einsum("mij,jd->imd", probs_low, value_head, preferred_element_type=F32)
    attn_out = attn_out.astype(BF16).reshape(4, 2, seq, heads * HD)
    attn_out = jnp.concatenate([attn_out, attn_out], axis=0)
    attn_out = lax.dynamic_slice(attn_out, (y, 0, 0, 0), (4,) + attn_out.shape[1:])
    attn_out = jnp.where(low == 0, attn_out, attn_out[:, ::-1])
    out_near = jnp.stack([attn_out, sibling(attn_out)], axis=2)
    out_other = across(out_near)

    outs = [out_near[:, 0], out_other[:, 0], out_other[:, 1], out_near[:, 1]]
    outs = [o.reshape(4 * 2 * seq, heads * HD) for o in outs]

    def partial(block):
        p = nt(block, weight).reshape(4, 2, seq, heads * HD)
        return p[:, 0] + sibling(p[:, 1].astype(BF16)).astype(F32)

    sums = [partial(b) for b in blocks]
    to_row = jnp.stack([sums[1], sums[2]], axis=1).astype(BF16)
    attn_grad = jnp.stack([sums[0], sums[3]], axis=1) + across(to_row).astype(F32)
    attn_grad = attn_grad.astype(BF16)
    attn_grad = jnp.where(low == 0, attn_grad, attn_grad[:, ::-1])
    attn_grad = jnp.concatenate([attn_grad, attn_grad], axis=0)
    attn_grad = lax.dynamic_slice(attn_grad, ((4 - y) % 4, 0, 0, 0), (4,) + attn_grad.shape[1:])

    def wgrad(k):
        cols = slice(k * width, (k + 1) * width)
        return sum(tn(o, b[:, cols]) for o, b in zip(outs, blocks))

    far = wgrad(2).astype(BF16)
    ahead = wgrad(1)
    behind = wgrad(3)
    up_part = z_up(far[:half])
    down_part = z_down(far[half:])
    ahead_free = z_up(ahead[half:].astype(BF16))
    behind_free = z_down(behind[:half].astype(BF16))
    ahead_sum = z_up((ahead[:half] + up_part.astype(F32)).astype(BF16))
    behind_sum = z_down((behind[half:] + down_part.astype(F32)).astype(BF16))
    mine = wgrad(0)
    weight_grad = mine + jnp.concatenate(
        [ahead_sum.astype(F32) + behind_free.astype(F32), ahead_free.astype(F32) + behind_sum.astype(F32)], axis=0
    )

    grad_heads = attn_grad.reshape(length, heads, HD)
    prob_grad = jnp.einsum("imd,jd->mij", grad_heads, value_head, preferred_element_type=F32)
    delta = jnp.sum(probs * prob_grad, axis=-1, keepdims=True)
    score_grad = (score_scale * probs * (prob_grad - delta)).astype(BF16)
    query_grad = jnp.einsum("mij,jd->imd", score_grad, key_head, preferred_element_type=F32)
    query_grad = query_grad.astype(BF16).reshape(1, length, heads * HD)
    key_grad = jnp.einsum("mij,imd->jd", score_grad, query_heads, preferred_element_type=F32)
    value_grad = jnp.einsum("mij,imd->jd", probs_low, grad_heads, preferred_element_type=F32)
    return (query_grad, key_grad.astype(BF16)[None], value_grad.astype(BF16)[None], weight_grad)


def solution(mesh):
    in_specs = (
        P("dp", None, "tensor"),
        P("dp", None, "tensor"),
        P("dp", None, "tensor"),
        P("dp", "tensor"),
        P("dp", None),
        P("dp", "tensor", None),
        P("tensor", "dp"),
    )
    out_specs = (
        P("dp", None, "tensor"),
        P("dp", None, "tensor"),
        P("dp", None, "tensor"),
        P("tensor", "dp"),
    )
    return jax.shard_map(shards, mesh=mesh, in_specs=in_specs, out_specs=out_specs, check_vma=False)
```

```python
import functools

import jax
import jax.numpy as jnp
from jax import lax
from jax.experimental import pallas as pl
from jax.experimental.pallas import tpu as pltpu
from jax.sharding import PartitionSpec as P

HD = 128
F32 = jnp.float32
BF16 = jnp.bfloat16
SCALE = HD ** (-0.5)
LIGHT = pl.CostEstimate(flops=0, bytes_accessed=0, transcendentals=0)
VMEM_MOST = 60 * 1024 * 1024


def by_dp(step):
    return [(i, step(i)) for i in range(16)]


def by_tensor(step):
    return [(i, step(i)) for i in range(8)]


SIBLING = by_dp(lambda i: i ^ 1)
ACROSS = by_dp(lambda i: i ^ 2)
PAIR = by_tensor(lambda i: i ^ 1)
Y_UP = by_tensor(lambda i: (i + 2) % 8)
Y_DOWN = by_tensor(lambda i: (i - 2) % 8)
Z_GROUPS = [[z * 4 + j for z in range(4)] for j in range(4)]


def sibling(x):
    return lax.ppermute(x, "dp", SIBLING)


def across(x):
    return lax.ppermute(x, "dp", ACROSS)


def pair(x):
    return lax.ppermute(x, "tensor", PAIR)


def y_up(x):
    return lax.ppermute(x, "tensor", Y_UP)


def y_down(x):
    return lax.ppermute(x, "tensor", Y_DOWN)


def nn(a, b):
    return lax.dot_general(a, b, (((1,), (0,)), ((), ())), preferred_element_type=F32)


def nt(a, b):
    return lax.dot_general(a, b, (((1,), (1,)), ((), ())), preferred_element_type=F32)


def params():
    return pltpu.CompilerParams(vmem_limit_bytes=VMEM_MOST, dimension_semantics=("arbitrary",))


SMEM = functools.partial(pl.BlockSpec, memory_space=pltpu.SMEM)


def whole(shape):
    return pl.BlockSpec(shape, lambda i: (0,) * len(shape))


def prep_kernel(place, margins, segs, up, own, to_sibling, to_across):
    h, c = place[2], place[3]
    seg = segs[...]
    margin = jnp.full(seg.shape, margins[0, 0], F32)
    for p in range(1, margins.shape[1]):
        margin = jnp.where((seg >> 1) == p, margins[0, p], margin)
    factor = jax.nn.sigmoid(-margin) * jnp.where((seg & 1) == 0, -1.0, 1.0)
    width = own.shape[1]
    factor = jnp.concatenate([factor] * (width // factor.shape[1]), axis=1)

    def grad(hh, cc):
        start = pl.multiple_of((hh * 2 + cc) * width, width)
        return (up[:, pl.ds(start, width)].astype(F32) * factor).astype(BF16)

    own[...] = grad(h, c)
    to_sibling[...] = grad(h, 1 - c)
    to_across[0] = grad(1 - h, c)
    to_across[1] = grad(1 - h, 1 - c)


def prep(place, margins, segs, up):
    seq, model = up.shape
    width = model // 16
    shape = jax.ShapeDtypeStruct((seq, 4 * width), BF16)
    col = pl.BlockSpec((seq, width), lambda i: (0, i))
    return pl.pallas_call(
        prep_kernel,
        grid=(4,),
        in_specs=[SMEM(), SMEM(), whole(segs.shape), pl.BlockSpec((seq, 4 * width), lambda i: (0, i))],
        out_specs=[col, col, pl.BlockSpec((2, seq, width), lambda i: (0, 0, i))],
        out_shape=[shape, shape, jax.ShapeDtypeStruct((2, seq, 4 * width), BF16)],
        compiler_params=params(),
        cost_estimate=LIGHT,
        name="prep",
    )(place, margins, segs, up)


def key_range(block):
    return max(0, block - 2) * HD, (block + 1) * HD


def two_heads(ref, block):
    rows = slice(block * HD, (block + 1) * HD)
    return jnp.concatenate([ref[rows, :HD], ref[rows, HD:]], axis=0)


def twice(x):
    return jnp.concatenate([x, x], axis=1)


def forward_kernel(place, segs, q, k, v, out, stats, bias, v_t):
    y, low = place[0], place[1]
    blocks = q.shape[0] // HD

    @pl.when(pl.program_id(0) == 0)
    def _():
        v_t[...] = v[...].astype(F32).T.astype(BF16)
        for b in range(blocks):
            first, last = key_range(b)
            of_query = segs[b * HD : (b + 1) * HD, :].astype(F32).T[:1]
            of_key = segs[first:last, :].astype(F32)
            shape = (last - first, HD)
            query_at = lax.broadcasted_iota(jnp.int32, shape, 1) + b * HD
            key_at = lax.broadcasted_iota(jnp.int32, shape, 0) + first
            seen = (of_key == of_query) & (key_at <= query_at)
            bias[b, : last - first] = jnp.where(seen, 0.0, -1e30)

    for b in range(blocks):
        first, last = key_range(b)
        q2 = two_heads(q, b)
        s = nt(k[first:last], q2) * SCALE + twice(bias[b, : last - first])
        highest = jnp.max(s, axis=0, keepdims=True)
        e = jnp.exp(s - highest)
        inverse = 1.0 / jnp.sum(e, axis=0, keepdims=True)
        stats[0, b : b + 1] = highest
        stats[0, blocks + b : blocks + b + 1] = inverse
        a = nn(v_t[:, first:last], (e * inverse).astype(BF16))
        at = pl.multiple_of(lax.rem(b - y + 4, 4) * HD, HD)
        for i in range(2):
            x = a[:, i * HD : (i + 1) * HD]
            x = jnp.where(low == 0, x, pltpu.roll(x, HD // 2, 1))
            out[i * HD : (i + 1) * HD, pl.ds(at, HD)] = x.astype(BF16)


def forward(place, segs, q, k, v):
    length, wide = q.shape
    pairs, blocks = wide // (2 * HD), length // HD
    bias_shape = (blocks, 3 * HD, HD)
    return pl.pallas_call(
        forward_kernel,
        grid=(pairs,),
        in_specs=[
            SMEM(),
            whole(segs.shape),
            pl.BlockSpec((length, 2 * HD), lambda i: (0, i)),
            whole(k.shape),
            whole(v.shape),
        ],
        out_specs=[
            pl.BlockSpec((2 * HD, length), lambda i: (i, 0)),
            pl.BlockSpec((1, 2 * blocks, 2 * HD), lambda i: (i, 0, 0)),
            whole(bias_shape),
        ],
        out_shape=[
            jax.ShapeDtypeStruct((wide, length), BF16),
            jax.ShapeDtypeStruct((pairs, 2 * blocks, 2 * HD), F32),
            jax.ShapeDtypeStruct(bias_shape, F32),
        ],
        scratch_shapes=[pltpu.VMEM((HD, length), BF16)],
        compiler_params=params(),
        cost_estimate=LIGHT,
        name="attend",
    )(place, segs, q, k, v)


def backward_kernel(place, q, k, v, stats, bias, *rest):
    terms, (dq, dk, dv, k_t, dk_sum, dv_sum) = rest[:6], rest[6:]
    y, low = place[0], place[1]
    blocks = q.shape[0] // HD
    half = HD // 2

    @pl.when(pl.program_id(0) == 0)
    def _():
        k_t[...] = k[...].astype(F32).T.astype(BF16)
        dk_sum[...] = jnp.zeros_like(dk_sum)
        dv_sum[...] = jnp.zeros_like(dv_sum)

    for b in range(blocks):
        first, last = key_range(b)
        rows = pl.ds(pl.multiple_of(lax.rem(b - y + 4, 4) * half, half), half)
        same = terms[0][rows] + terms[1][rows].astype(F32) + terms[2][rows].astype(F32)
        flip = terms[3][rows] + terms[4][rows].astype(F32) + terms[5][rows].astype(F32)
        grad = jnp.concatenate([jnp.where(low == 0, same, flip), jnp.where(low == 0, flip, same)], axis=0).astype(BF16)
        grad = jnp.concatenate([grad[:, :HD], grad[:, HD:]], axis=0)
        q2 = two_heads(q, b)
        s = nt(k[first:last], q2) * SCALE + twice(bias[b, : last - first])
        p = jnp.exp(s - stats[0, b : b + 1]) * stats[0, blocks + b : blocks + b + 1]
        dp = nt(v[first:last], grad)
        delta = jnp.sum(p * dp, axis=0, keepdims=True)
        ds = (SCALE * p * (dp - delta)).astype(BF16)
        dv_sum[first:last] += nn(p.astype(BF16), grad)
        dk_sum[first:last] += nn(ds, q2)
        x = nn(k_t[:, first:last], ds)
        for i in range(2):
            dq[b * HD : (b + 1) * HD, i * HD : (i + 1) * HD] = x[:, i * HD : (i + 1) * HD].T.astype(BF16)

    @pl.when(pl.program_id(0) == pl.num_programs(0) - 1)
    def _():
        dk[...] = dk_sum[...].astype(BF16)
        dv[...] = dv_sum[...].astype(BF16)


def backward(place, q, k, v, stats, bias, terms):
    length, wide = q.shape
    pairs, blocks = wide // (2 * HD), length // HD
    two = pl.BlockSpec((length, 2 * HD), lambda i: (0, i))
    return pl.pallas_call(
        backward_kernel,
        grid=(pairs,),
        in_specs=[
            SMEM(),
            two,
            whole(k.shape),
            whole(v.shape),
            pl.BlockSpec((1, 2 * blocks, 2 * HD), lambda i: (i, 0, 0)),
            whole(bias.shape),
        ]
        + [pl.BlockSpec((length // 2, 2 * HD), lambda i: (0, i))] * 6,
        out_specs=[two, whole(k.shape), whole(v.shape)],
        out_shape=[jax.ShapeDtypeStruct(x.shape, BF16) for x in (q, k, v)],
        scratch_shapes=[pltpu.VMEM((HD, length), BF16), pltpu.VMEM(k.shape, F32), pltpu.VMEM(v.shape, F32)],
        compiler_params=params(),
        cost_estimate=LIGHT,
        name="attend_grad",
    )(place, q, k, v, stats, bias, *terms)


def partial_kernel(*refs):
    blocks, (weight, keep, give, x) = refs[:4], refs[4:]
    seq = blocks[0].shape[1]
    half = 4 * seq
    width = weight.shape[2]

    @pl.when(pl.program_id(0) == 0)
    def _():
        for i in range(2):
            for j, block in enumerate(blocks):
                x[i * half + j * seq : i * half + (j + 1) * seq] = block[i]

    total = nt(x[:, :width], weight[0])
    for j in range(1, 4):
        total += nt(x[:, j * width : (j + 1) * width], weight[j])
    keep[...] = total[:half]
    give[...] = total[half:].astype(BF16)


def partial(blocks, weight):
    _, seq, cols = blocks[0].shape
    heads = weight.shape[1]
    tile = heads // 4
    out = pl.BlockSpec((4 * seq, tile), lambda i: (0, i))
    return pl.pallas_call(
        partial_kernel,
        grid=(4,),
        in_specs=[whole(blocks[0].shape)] * 4 + [pl.BlockSpec((4, tile, cols // 4), lambda i: (0, i, 0))],
        out_specs=[out, out],
        out_shape=[jax.ShapeDtypeStruct((4 * seq, heads), F32), jax.ShapeDtypeStruct((4 * seq, heads), BF16)],
        scratch_shapes=[pltpu.VMEM((8 * seq, cols), BF16)],
        compiler_params=params(),
        cost_estimate=LIGHT,
        name="partial_grad",
    )(*blocks, weight)


def wgrad_kernel(has_start, *refs):
    same, flip, outs = refs[:4], refs[4:8], refs[8:10]
    start = refs[10] if has_start else None
    out, x = refs[-2:]
    seq = same[0].shape[1]
    for i in range(2):
        for j in range(4):
            at = (i * 8 + j * 2) * seq
            x[at : at + seq] = same[j][i]
            x[at + seq : at + 2 * seq] = flip[j][i]
    half = 8 * seq
    tile = 256
    for m in range(0, out.shape[1], tile):
        total = nn(outs[0][m : m + tile], x[:half]) + nn(outs[1][m : m + tile], x[half:])
        if has_start:
            total += start[0, m : m + tile]
        out[0, m : m + tile] = total.astype(out.dtype)


def wgrad(same, flip, outs, start):
    _, seq, cols = same[0].shape
    heads = outs[0].shape[0]
    width = cols // 4
    col = pl.BlockSpec((2, seq, width), lambda i: (0, 0, i))
    result = pl.BlockSpec((1, heads, width), lambda i: (i, 0, 0))
    return pl.pallas_call(
        functools.partial(wgrad_kernel, start is not None),
        grid=(4,),
        in_specs=[col] * 8 + [whole(outs[0].shape)] * 2 + ([] if start is None else [result]),
        out_specs=result,
        out_shape=jax.ShapeDtypeStruct((4, heads, width), F32 if start is None else BF16),
        scratch_shapes=[pltpu.VMEM((16 * seq, width), BF16)],
        compiler_params=params(),
        cost_estimate=LIGHT,
        name="weight_grad",
    )(*same, *flip, *outs, *([] if start is None else [start]))


def named(name, fn, x):
    with jax.named_scope("t_" + name):
        return fn(x)


def after(x, *others):
    return lax.optimization_barrier((x, *others))[0]


def gather_ids(ids):
    low = lax.axis_index("tensor") % 2
    y = lax.axis_index("tensor") // 2
    partner = named("ids_pair", pair, ids)
    both = jnp.where(low == 0, jnp.stack([ids, partner]), jnp.stack([partner, ids]))
    behind = named("ids_up", y_up, both)
    ahead = named("ids_down", y_down, both)
    far = named("ids_far", lambda x: lax.ppermute(x, "tensor", by_tensor(lambda i: (i + 4) % 8)), both)
    ring = jnp.stack([both, ahead, far, behind] * 2).reshape(8, -1)
    return lax.dynamic_slice(ring, ((4 - y) % 4, 0), (4, ring.shape[1])).reshape(-1)


def shards(query_states, key_states, value_states, segment_ids, pair_margins, upstream, out_weight):
    d = lax.axis_index("dp")
    t = lax.axis_index("tensor")
    place = jnp.stack([t // 2, t % 2, (d // 2) % 2, d % 2]).astype(jnp.int32)
    query, key, value = query_states[0], key_states[0], value_states[0]

    segs = jnp.broadcast_to(segment_ids[0][:, None], (segment_ids.shape[1], HD))
    own, to_sibling, to_across = prep(place, pair_margins, segs, upstream[0])
    heads, width = out_weight.shape
    weight = lax.all_gather(out_weight, "dp", axis=0, tiled=True, axis_index_groups=Z_GROUPS).reshape(4, heads, width)

    from_sibling = named("near_sibling", sibling, to_sibling)
    near = jnp.stack([own, from_sibling])
    from_across = named("other_across", across, to_across)
    other = jnp.stack([from_across[0], named("other_sibling", sibling, from_across[1])])
    near_pair = named("near_pair", pair, near)
    other_pair = named("other_pair", pair, other)

    def to_row(name, blocks):
        keep, give = partial(blocks, weight)
        total = (keep + named(name + "_sibling", sibling, give).astype(F32)).astype(BF16)
        return named(name + "_across", across, total), total

    def for_row(name, blocks):
        keep, give = partial(blocks, weight)
        return keep, named(name + "_sibling", sibling, give)

    n, o, p, q = near, other, other_pair, near_pair
    n_up, n_down = named("n_up", y_up, n), named("n_down", y_down, n)

    ids = gather_ids(after(segment_ids[0], from_sibling))
    whole_segs = jnp.broadcast_to(ids[:, None], (ids.shape[0], HD))
    attn_out, stats, bias = forward(place, whole_segs, after(query, other, n_up, n_down), key, value)
    out_across = named("out_across", across, attn_out)

    n_far, o_down = named("n_far", y_up, after(n_up, n_down)), named("o_down", y_down, after(o, q, ids))
    o_up, o_far = named("o_up", y_up, after(o, n_up, n_down, p, attn_out)), named("o_far", y_down, after(o_down, attn_out))
    p = after(p, n_far, o_down)
    p_up, p_down = named("p_up", y_up, p), named("p_down", y_down, p)
    terms_same = for_row("sum_near", [n, n_down, n_far, after(n_up, o_up, o_far)])
    p_far, q_down = named("p_far", y_up, after(p_up, terms_same[0])), named("q_down", y_down, after(q, o_up, o_far, terms_same[0]))
    sent_same, sum_other = to_row("sum_other", [o, o_down, o_far, after(o_up, p_up, p_down)])
    q_up, q_far = named("q_up", y_up, after(q, p_up, p_down, sum_other)), named("q_far", y_down, after(q_down, sum_other))
    near_blocks = [n, n_down, n_far, n_up]
    other_blocks = [o, o_down, o_far, o_up]
    other_pair_blocks = [p, p_down, p_far, p_up]
    near_pair_blocks = [q, q_down, q_far, q_up]
    sent_flip, sum_other_pair = to_row("sum_other_pair", [p, p_down, after(p_far, q_down), p_up])
    out_near = named("out_near", sibling, after(attn_out, o_up, o_far))
    out_other = named("out_other", sibling, after(out_across, o_up, o_far))
    first = wgrad(other_blocks, other_pair_blocks, (out_across, after(out_other, sum_other_pair)), None)
    total = wgrad(near_blocks, near_pair_blocks, (attn_out, out_near), after(first, sent_same))
    terms_flip = for_row("sum_near_pair", near_pair_blocks)
    terms = [*terms_same, sent_same, *terms_flip, sent_flip]
    weight_grad = lax.psum_scatter(
        total.reshape(4 * heads, width), "dp", scatter_dimension=0, tiled=True, axis_index_groups=Z_GROUPS
    )
    dq, dk, dv = backward(place, query, key, value, stats, bias, terms)
    return (dq[None], dk[None], dv[None], weight_grad.astype(F32))


def solution(mesh):
    in_specs = (
        P("dp", None, "tensor"),
        P("dp", None, "tensor"),
        P("dp", None, "tensor"),
        P("dp", "tensor"),
        P("dp", None),
        P("dp", "tensor", None),
        P("tensor", "dp"),
    )
    out_specs = (
        P("dp", None, "tensor"),
        P("dp", None, "tensor"),
        P("dp", None, "tensor"),
        P("tensor", "dp"),
    )
    return jax.shard_map(shards, mesh=mesh, in_specs=in_specs, out_specs=out_specs, check_vma=False)
```

```python
import functools

import jax
import jax.numpy as jnp
from jax import lax
from jax.experimental import pallas as pl
from jax.experimental.pallas import tpu as pltpu
from jax.sharding import PartitionSpec as P

HD = 128
F32 = jnp.float32
BF16 = jnp.bfloat16
SCALE = HD ** (-0.5)
LIGHT = pl.CostEstimate(flops=0, bytes_accessed=0, transcendentals=0)
VMEM_MOST = 60 * 1024 * 1024


def by_dp(step):
    return [(i, step(i)) for i in range(16)]


def by_tensor(step):
    return [(i, step(i)) for i in range(8)]


SIBLING = by_dp(lambda i: i ^ 1)
ACROSS = by_dp(lambda i: i ^ 2)
DIAGONAL = by_dp(lambda i: i ^ 3)
PAIR = by_tensor(lambda i: i ^ 1)
Y_UP = by_tensor(lambda i: (i + 2) % 8)
Y_DOWN = by_tensor(lambda i: (i - 2) % 8)
Z_GROUPS = [[z * 4 + j for z in range(4)] for j in range(4)]


def sibling(x):
    return lax.ppermute(x, "dp", SIBLING)


def across(x):
    return lax.ppermute(x, "dp", ACROSS)


def diagonal(x):
    return lax.ppermute(x, "dp", DIAGONAL)


def pair(x):
    return lax.ppermute(x, "tensor", PAIR)


def y_up(x):
    return lax.ppermute(x, "tensor", Y_UP)


def y_down(x):
    return lax.ppermute(x, "tensor", Y_DOWN)


def nn(a, b):
    return lax.dot_general(a, b, (((1,), (0,)), ((), ())), preferred_element_type=F32)


def nt(a, b):
    return lax.dot_general(a, b, (((1,), (1,)), ((), ())), preferred_element_type=F32)


def params():
    return pltpu.CompilerParams(vmem_limit_bytes=VMEM_MOST, dimension_semantics=("arbitrary",))


SMEM = functools.partial(pl.BlockSpec, memory_space=pltpu.SMEM)


def whole(shape):
    return pl.BlockSpec(shape, lambda i: (0,) * len(shape))


def prep_kernel(place, margins, segs, up, own, to_sibling, to_across, to_diagonal):
    h, c = place[2], place[3]
    seg = segs[...]
    margin = jnp.full(seg.shape, margins[0, 0], F32)
    for p in range(1, margins.shape[1]):
        margin = jnp.where((seg >> 1) == p, margins[0, p], margin)
    factor = jax.nn.sigmoid(-margin) * jnp.where((seg & 1) == 0, -1.0, 1.0)
    width = own.shape[2]
    factor = jnp.concatenate([factor] * (width // factor.shape[1]), axis=1)

    def put(ref, hh, cc):
        for e in range(2):
            start = pl.multiple_of((hh * 2 + cc) * 2 * width, 2 * width) + e * width
            ref[e] = (up[:, pl.ds(start, width)].astype(F32) * factor).astype(BF16)

    put(own, h, c)
    put(to_sibling, h, 1 - c)
    put(to_across, 1 - h, c)
    put(to_diagonal, 1 - h, 1 - c)


def prep(place, margins, segs, up):
    seq, model = up.shape
    width = model // 32
    shape = jax.ShapeDtypeStruct((2, seq, 4 * width), BF16)
    col = pl.BlockSpec((2, seq, width), lambda i: (0, 0, i))
    return pl.pallas_call(
        prep_kernel,
        grid=(4,),
        in_specs=[SMEM(), SMEM(), whole(segs.shape), pl.BlockSpec((seq, 8 * width), lambda i: (0, i))],
        out_specs=[col] * 4,
        out_shape=[shape] * 4,
        compiler_params=params(),
        cost_estimate=LIGHT,
        name="prep",
    )(place, margins, segs, up)


def key_range(block):
    return max(0, block - 2) * HD, (block + 1) * HD


def two_heads(ref, block):
    rows = slice(block * HD, (block + 1) * HD)
    return jnp.concatenate([ref[rows, :HD], ref[rows, HD:]], axis=0)


def twice(x):
    return jnp.concatenate([x, x], axis=1)


def forward_kernel(place, segs, q, k, v, out, stats, bias, v_t):
    y, low = place[0], place[1]
    blocks = q.shape[0] // HD

    @pl.when(pl.program_id(0) == 0)
    def _():
        v_t[...] = v[...].astype(F32).T.astype(BF16)
        for b in range(blocks):
            first, last = key_range(b)
            of_query = segs[b * HD : (b + 1) * HD, :].astype(F32).T[:1]
            of_key = segs[first:last, :].astype(F32)
            shape = (last - first, HD)
            query_at = lax.broadcasted_iota(jnp.int32, shape, 1) + b * HD
            key_at = lax.broadcasted_iota(jnp.int32, shape, 0) + first
            seen = (of_key == of_query) & (key_at <= query_at)
            bias[b, : last - first] = jnp.where(seen, 0.0, -1e30)

    for b in range(blocks):
        first, last = key_range(b)
        q2 = two_heads(q, b)
        s = nt(k[first:last], q2) * SCALE + twice(bias[b, : last - first])
        highest = jnp.max(s, axis=0, keepdims=True)
        e = jnp.exp(s - highest)
        inverse = 1.0 / jnp.sum(e, axis=0, keepdims=True)
        stats[0, b : b + 1] = highest
        stats[0, blocks + b : blocks + b + 1] = inverse
        a = nn(v_t[:, first:last], (e * inverse).astype(BF16))
        at = pl.multiple_of(lax.rem(b - y + 4, 4) * HD, HD)
        for i in range(2):
            x = a[:, i * HD : (i + 1) * HD]
            x = jnp.where(low == 0, x, pltpu.roll(x, HD // 2, 1))
            out[i * HD : (i + 1) * HD, pl.ds(at, HD)] = x.astype(BF16)


def forward(place, segs, q, k, v):
    length, wide = q.shape
    pairs, blocks = wide // (2 * HD), length // HD
    bias_shape = (blocks, 3 * HD, HD)
    return pl.pallas_call(
        forward_kernel,
        grid=(pairs,),
        in_specs=[
            SMEM(),
            whole(segs.shape),
            pl.BlockSpec((length, 2 * HD), lambda i: (0, i)),
            whole(k.shape),
            whole(v.shape),
        ],
        out_specs=[
            pl.BlockSpec((2 * HD, length), lambda i: (i, 0)),
            pl.BlockSpec((1, 2 * blocks, 2 * HD), lambda i: (i, 0, 0)),
            whole(bias_shape),
        ],
        out_shape=[
            jax.ShapeDtypeStruct((wide, length), BF16),
            jax.ShapeDtypeStruct((pairs, 2 * blocks, 2 * HD), F32),
            jax.ShapeDtypeStruct(bias_shape, F32),
        ],
        scratch_shapes=[pltpu.VMEM((HD, length), BF16)],
        compiler_params=params(),
        cost_estimate=LIGHT,
        name="attend",
    )(place, segs, q, k, v)


def backward_kernel(place, q, k, v, stats, bias, *rest):
    terms, (dq, dk, dv, k_t, dk_sum, dv_sum) = rest[:6], rest[6:]
    y, low = place[0], place[1]
    blocks = q.shape[0] // HD
    half = HD // 2

    @pl.when(pl.program_id(0) == 0)
    def _():
        k_t[...] = k[...].astype(F32).T.astype(BF16)
        dk_sum[...] = jnp.zeros_like(dk_sum)
        dv_sum[...] = jnp.zeros_like(dv_sum)

    for b in range(blocks):
        first, last = key_range(b)
        rows = pl.ds(pl.multiple_of(lax.rem(b - y + 4, 4) * half, half), half)
        same = terms[0][rows] + terms[1][rows].astype(F32) + terms[2][rows].astype(F32)
        flip = terms[3][rows] + terms[4][rows].astype(F32) + terms[5][rows].astype(F32)
        grad = jnp.concatenate([jnp.where(low == 0, same, flip), jnp.where(low == 0, flip, same)], axis=0).astype(BF16)
        grad = jnp.concatenate([grad[:, :HD], grad[:, HD:]], axis=0)
        q2 = two_heads(q, b)
        s = nt(k[first:last], q2) * SCALE + twice(bias[b, : last - first])
        p = jnp.exp(s - stats[0, b : b + 1]) * stats[0, blocks + b : blocks + b + 1]
        dp = nt(v[first:last], grad)
        delta = jnp.sum(p * dp, axis=0, keepdims=True)
        ds = (SCALE * p * (dp - delta)).astype(BF16)
        dv_sum[first:last] += nn(p.astype(BF16), grad)
        dk_sum[first:last] += nn(ds, q2)
        x = nn(k_t[:, first:last], ds)
        for i in range(2):
            dq[b * HD : (b + 1) * HD, i * HD : (i + 1) * HD] = x[:, i * HD : (i + 1) * HD].T.astype(BF16)

    @pl.when(pl.program_id(0) == pl.num_programs(0) - 1)
    def _():
        dk[...] = dk_sum[...].astype(BF16)
        dv[...] = dv_sum[...].astype(BF16)


def backward(place, q, k, v, stats, bias, terms):
    length, wide = q.shape
    pairs, blocks = wide // (2 * HD), length // HD
    two = pl.BlockSpec((length, 2 * HD), lambda i: (0, i))
    return pl.pallas_call(
        backward_kernel,
        grid=(pairs,),
        in_specs=[
            SMEM(),
            two,
            whole(k.shape),
            whole(v.shape),
            pl.BlockSpec((1, 2 * blocks, 2 * HD), lambda i: (i, 0, 0)),
            whole(bias.shape),
        ]
        + [pl.BlockSpec((length // 2, 2 * HD), lambda i: (0, i))] * 6,
        out_specs=[two, whole(k.shape), whole(v.shape)],
        out_shape=[jax.ShapeDtypeStruct(x.shape, BF16) for x in (q, k, v)],
        scratch_shapes=[pltpu.VMEM((HD, length), BF16), pltpu.VMEM(k.shape, F32), pltpu.VMEM(v.shape, F32)],
        compiler_params=params(),
        cost_estimate=LIGHT,
        name="attend_grad",
    )(place, q, k, v, stats, bias, *terms)


def partial_kernel(*refs):
    pieces, (weight, keep, give, x) = refs[:8], refs[8:]
    _, _, seq, cols = pieces[0].shape
    half = 4 * seq
    width = weight.shape[2] // 2

    @pl.when(pl.program_id(0) == 0)
    def _():
        for e in range(2):
            for i in range(2):
                for j in range(4):
                    at = i * half + j * seq
                    x[at : at + seq, e * cols : (e + 1) * cols] = pieces[e * 4 + j][0, i]

    w = jnp.concatenate([weight[j, :, e * width : (e + 1) * width] for e in range(2) for j in range(4)], axis=1)
    total = nt(x[...], w)
    keep[...] = total[:half]
    give[...] = total[half:].astype(BF16)


def partial(pieces, weight):
    _, _, seq, cols = pieces[0][0].shape
    heads = weight.shape[1]
    tile = heads // 2
    out = pl.BlockSpec((4 * seq, tile), lambda i: (0, i))

    def spec(index):
        return pl.BlockSpec((1, 2, seq, cols), lambda i: (index, 0, 0, 0))

    return pl.pallas_call(
        partial_kernel,
        grid=(2,),
        in_specs=[spec(index) for _, index in pieces] + [pl.BlockSpec((4, tile, cols // 2), lambda i: (0, i, 0))],
        out_specs=[out, out],
        out_shape=[jax.ShapeDtypeStruct((4 * seq, heads), F32), jax.ShapeDtypeStruct((4 * seq, heads), BF16)],
        scratch_shapes=[pltpu.VMEM((8 * seq, 2 * cols), BF16)],
        compiler_params=params(),
        cost_estimate=LIGHT,
        name="partial_grad",
    )(*[x for x, _ in pieces], weight)


def wgrad_kernel(*refs):
    near, other, flip, outs, (out, x) = refs[:4], refs[4:8], refs[8:12], refs[12:16], refs[16:]
    _, _, seq, cols = near[0].shape
    length = 8 * seq
    for i in range(2):
        for j in range(4):
            for row, block in ((i, near[j][0, i]), (2 + i, other[j][0, i])):
                at = row * length + 2 * j * seq
                x[at : at + seq] = block
            for row, block in ((i, flip[j][0, i]), (2 + i, flip[j][1, i])):
                at = row * length + (2 * j + 1) * seq
                x[at : at + seq] = block
    tile = 256
    width = out.shape[2]
    for m in range(0, out.shape[1], tile):
        total = nn(outs[0][m : m + tile], x[:length])
        for r in range(1, 4):
            total += nn(outs[r][m : m + tile], x[r * length : (r + 1) * length])
        for k in range(cols // width):
            out[k, m : m + tile] = total[:, k * width : (k + 1) * width].astype(BF16)


def wgrad(half, near, other, flip, outs):
    _, _, seq, cols = near[0].shape
    heads = outs[0].shape[0]
    wide = cols // 2
    same = pl.BlockSpec((1, 2, seq, wide), lambda i: (half, 0, 0, i))
    return pl.pallas_call(
        wgrad_kernel,
        grid=(2,),
        in_specs=[same] * 8 + [pl.BlockSpec((2, 2, seq, wide), lambda i: (0, 0, 0, i))] * 4 + [whole(outs[0].shape)] * 4,
        out_specs=pl.BlockSpec((2, heads, wide // 2), lambda i: (i, 0, 0)),
        out_shape=jax.ShapeDtypeStruct((4, heads, wide // 2), BF16),
        scratch_shapes=[pltpu.VMEM((32 * seq, wide), BF16)],
        compiler_params=params(),
        cost_estimate=LIGHT,
        name="weight_grad",
    )(*near, *other, *flip, *outs)


def named(name, fn, x):
    with jax.named_scope("t_" + name):
        return fn(x)


def after(x, *others):
    return lax.optimization_barrier((x, *others))[0]


def shards(query_states, key_states, value_states, segment_ids, pair_margins, upstream, out_weight):
    d = lax.axis_index("dp")
    t = lax.axis_index("tensor")
    y, low = t // 2, t % 2
    place = jnp.stack([y, low, (d // 2) % 2, d % 2]).astype(jnp.int32)
    query, key, value = query_states[0], key_states[0], value_states[0]
    heads, width = out_weight.shape
    weight = lax.all_gather(out_weight, "dp", axis=0, tiled=True, axis_index_groups=Z_GROUPS).reshape(4, heads, width)

    ids = segment_ids[0]
    partner = named("ids_pair", pair, ids)
    segs = jnp.broadcast_to(ids[:, None], (ids.shape[0], HD))
    own, to_sibling, to_across, to_diagonal = prep(place, pair_margins, segs, upstream[0])

    from_across = named("other_across", across, to_across)
    from_diagonal = named("other_diagonal", diagonal, to_diagonal)
    near = jnp.stack([own, named("near_sibling", sibling, after(to_sibling, partner))], axis=1)
    n_up, n_down = named("n_up", y_up, near), named("n_down", y_down, near)
    both = jnp.where(low == 0, jnp.stack([ids, partner]), jnp.stack([partner, ids]))
    both = after(both, near)
    ids_up = named("ids_up", y_up, both)
    ids_down = named("ids_down", y_down, both)
    ids_far = named("ids_far", lambda x: lax.ppermute(x, "tensor", by_tensor(lambda i: (i + 4) % 8)), both)
    ring = jnp.stack([both, ids_down, ids_far, ids_up] * 2).reshape(8, -1)
    ids = lax.dynamic_slice(ring, ((4 - y) % 4, 0), (4, ring.shape[1])).reshape(-1)
    whole_segs = jnp.broadcast_to(ids[:, None], (ids.shape[0], HD))

    other = jnp.stack([after(from_across, n_up, n_down, ids_up, ids_down, ids_far), from_diagonal], axis=1)
    flips = [named("pair_%d" % e, pair, jnp.stack([near[e], other[e]])) for e in range(2)]

    def to_row(name, pieces):
        keep, give = partial(pieces, weight)
        total = (keep + named(name + "_sibling", sibling, give).astype(F32)).astype(BF16)
        return named(name + "_across", across, total), total

    def for_row(name, pieces):
        keep, give = partial(pieces, weight)
        return keep, named(name + "_sibling", sibling, give)

    n, o, p, q = near, other, flips[0], flips[1]
    attn_out, stats, bias = forward(place, whole_segs, after(query, other, n_up, n_down), key, value)
    out_across = named("out_across", across, after(attn_out, q))

    n_far, o_down = named("n_far", y_up, after(n_up, n_down)), named("o_down", y_down, after(o, ids))
    o_up, o_far = named("o_up", y_up, after(o, n_up, n_down, p, attn_out)), named("o_far", y_down, after(o_down, attn_out))
    p = after(p, n_far, o_down)
    p_up, p_down = named("p_up", y_up, p), named("p_down", y_down, p)
    near_blocks = [n, n_down, n_far, n_up]
    other_blocks = [o, o_down, o_far, o_up]
    terms_same = for_row("sum_near", [(x, e) for e in range(2) for x in [n, n_down, n_far, after(n_up, o_up, o_far)]])
    p_far = named("p_far", y_up, p_up)
    q_down = named("q_down", y_down, after(q, o_up, o_far))
    sent_same, sum_other = to_row("sum_other", [(x, e) for e in range(2) for x in [o, o_down, o_far, after(o_up, p_up, p_down)]])
    q_up, q_far = named("q_up", y_up, after(q, p_up, p_down)), named("q_far", y_down, q_down)
    out_near = named("out_near", sibling, after(attn_out, o_up, o_far))
    out_other = named("out_other", sibling, after(out_across, o_up, o_far))
    outs = (attn_out, out_near, out_across, out_other)
    flip_blocks = [[p, p_down, after(p_far, q_down), p_up], [q, q_down, q_far, q_up]]

    def sum_z(x):
        return lax.psum_scatter(
            x.reshape(4 * heads, width // 2), "dp", scatter_dimension=0, tiled=True, axis_index_groups=Z_GROUPS
        )

    first = wgrad(0, near_blocks, other_blocks, flip_blocks[0], (*outs[:3], after(out_other, sum_other, q_up)))
    first_sum = sum_z(first)

    def flipped(row):
        return [(x, row) for e in range(2) for x in flip_blocks[e]]

    sent_flip, sum_other_flip = to_row("sum_other_flip", flipped(1))
    last = wgrad(1, near_blocks, other_blocks, flip_blocks[1], (*outs[:3], after(out_other, sum_other_flip)))
    last_sum = sum_z(last)
    terms_flip = for_row("sum_near_flip", [(after(x, last) if i == 0 else x, r) for i, (x, r) in enumerate(flipped(0))])
    terms = [*terms_same, sent_same, *terms_flip, sent_flip]
    dq, dk, dv = backward(place, query, key, value, stats, bias, terms)
    weight_grad = jnp.concatenate([first_sum, last_sum], axis=1).astype(F32)
    return (dq[None], dk[None], dv[None], weight_grad)


def solution(mesh):
    in_specs = (
        P("dp", None, "tensor"),
        P("dp", None, "tensor"),
        P("dp", None, "tensor"),
        P("dp", "tensor"),
        P("dp", None),
        P("dp", "tensor", None),
        P("tensor", "dp"),
    )
    out_specs = (
        P("dp", None, "tensor"),
        P("dp", None, "tensor"),
        P("dp", None, "tensor"),
        P("tensor", "dp"),
    )
    return jax.shard_map(shards, mesh=mesh, in_specs=in_specs, out_specs=out_specs, check_vma=False)
```

```python
import functools

import jax
import jax.numpy as jnp
from jax import lax
from jax.experimental import pallas as pl
from jax.experimental.pallas import tpu as pltpu
from jax.sharding import PartitionSpec as P

HD = 128
F32 = jnp.float32
BF16 = jnp.bfloat16
SCALE = HD ** (-0.5)
LIGHT = pl.CostEstimate(flops=0, bytes_accessed=0, transcendentals=0)
VMEM_MOST = 60 * 1024 * 1024


def by_dp(step):
    return [(i, step(i)) for i in range(16)]


def by_tensor(step):
    return [(i, step(i)) for i in range(8)]


SIBLING = by_dp(lambda i: i ^ 1)
ACROSS = by_dp(lambda i: i ^ 2)
DIAGONAL = by_dp(lambda i: i ^ 3)
PAIR = by_tensor(lambda i: i ^ 1)
Y_UP = by_tensor(lambda i: (i + 2) % 8)
Y_DOWN = by_tensor(lambda i: (i - 2) % 8)
Z_GROUPS = [[z * 4 + j for z in range(4)] for j in range(4)]
Y_GROUPS = [[y * 2 + low for y in range(4)] for low in range(2)]


def sibling(x):
    return lax.ppermute(x, "dp", SIBLING)


def across(x):
    return lax.ppermute(x, "dp", ACROSS)


def diagonal(x):
    return lax.ppermute(x, "dp", DIAGONAL)


def pair(x):
    return lax.ppermute(x, "tensor", PAIR)


def y_up(x):
    return lax.ppermute(x, "tensor", Y_UP)


def y_down(x):
    return lax.ppermute(x, "tensor", Y_DOWN)


def nn(a, b):
    return lax.dot_general(a, b, (((1,), (0,)), ((), ())), preferred_element_type=F32)


def nt(a, b):
    return lax.dot_general(a, b, (((1,), (1,)), ((), ())), preferred_element_type=F32)


def params():
    return pltpu.CompilerParams(vmem_limit_bytes=VMEM_MOST, dimension_semantics=("arbitrary",))


SMEM = functools.partial(pl.BlockSpec, memory_space=pltpu.SMEM)


def whole(shape):
    return pl.BlockSpec(shape, lambda i: (0,) * len(shape))


def prep_kernel(place, margins, segs, up, own, to_sibling, to_across, to_diagonal):
    h, c = place[2], place[3]
    seg = segs[...]
    margin = jnp.full(seg.shape, margins[0, 0], F32)
    for p in range(1, margins.shape[1]):
        margin = jnp.where((seg >> 1) == p, margins[0, p], margin)
    factor = jax.nn.sigmoid(-margin) * jnp.where((seg & 1) == 0, -1.0, 1.0)
    width = own.shape[2]
    factor = jnp.concatenate([factor] * (width // factor.shape[1]), axis=1)

    def put(ref, hh, cc):
        for e in range(2):
            start = pl.multiple_of((hh * 2 + cc) * 2 * width, 2 * width) + e * width
            ref[e] = (up[:, pl.ds(start, width)].astype(F32) * factor).astype(BF16)

    put(own, h, c)
    put(to_sibling, h, 1 - c)
    put(to_across, 1 - h, c)
    put(to_diagonal, 1 - h, 1 - c)


def prep(place, margins, segs, up):
    seq, model = up.shape
    width = model // 32
    shape = jax.ShapeDtypeStruct((2, seq, 4 * width), BF16)
    col = pl.BlockSpec((2, seq, width), lambda i: (0, 0, i))
    return pl.pallas_call(
        prep_kernel,
        grid=(4,),
        in_specs=[SMEM(), SMEM(), whole(segs.shape), pl.BlockSpec((seq, 8 * width), lambda i: (0, i))],
        out_specs=[col] * 4,
        out_shape=[shape] * 4,
        compiler_params=params(),
        cost_estimate=LIGHT,
        name="prep",
    )(place, margins, segs, up)


def key_range(block):
    return max(0, block - 2) * HD, (block + 1) * HD


def two_heads(ref, block):
    rows = slice(block * HD, (block + 1) * HD)
    return jnp.concatenate([ref[rows, :HD], ref[rows, HD:]], axis=0)


def twice(x):
    return jnp.concatenate([x, x], axis=1)


def forward_kernel(place, segs, q, k, v, out, stats, bias, v_t):
    y, low = place[0], place[1]
    blocks = q.shape[0] // HD

    @pl.when(pl.program_id(0) == 0)
    def _():
        v_t[...] = v[...].astype(F32).T.astype(BF16)
        for b in range(blocks):
            first, last = key_range(b)
            of_query = segs[b * HD : (b + 1) * HD, :].astype(F32).T[:1]
            of_key = segs[first:last, :].astype(F32)
            shape = (last - first, HD)
            query_at = lax.broadcasted_iota(jnp.int32, shape, 1) + b * HD
            key_at = lax.broadcasted_iota(jnp.int32, shape, 0) + first
            seen = (of_key == of_query) & (key_at <= query_at)
            bias[b, : last - first] = jnp.where(seen, 0.0, -1e30)

    for b in range(blocks):
        first, last = key_range(b)
        q2 = two_heads(q, b)
        s = nt(k[first:last], q2) * SCALE + twice(bias[b, : last - first])
        highest = jnp.max(s, axis=0, keepdims=True)
        e = jnp.exp(s - highest)
        inverse = 1.0 / jnp.sum(e, axis=0, keepdims=True)
        stats[0, b : b + 1] = highest
        stats[0, blocks + b : blocks + b + 1] = inverse
        a = nn(v_t[:, first:last], (e * inverse).astype(BF16))
        at = pl.multiple_of(lax.rem(b - y + 4, 4) * HD, HD)
        for i in range(2):
            x = a[:, i * HD : (i + 1) * HD]
            x = jnp.where(low == 0, x, pltpu.roll(x, HD // 2, 1))
            out[i * HD : (i + 1) * HD, pl.ds(at, HD)] = x.astype(BF16)


def forward(place, segs, q, k, v):
    length, wide = q.shape
    pairs, blocks = wide // (2 * HD), length // HD
    bias_shape = (blocks, 3 * HD, HD)
    return pl.pallas_call(
        forward_kernel,
        grid=(pairs,),
        in_specs=[
            SMEM(),
            whole(segs.shape),
            pl.BlockSpec((length, 2 * HD), lambda i: (0, i)),
            whole(k.shape),
            whole(v.shape),
        ],
        out_specs=[
            pl.BlockSpec((2 * HD, length), lambda i: (i, 0)),
            pl.BlockSpec((1, 2 * blocks, 2 * HD), lambda i: (i, 0, 0)),
            whole(bias_shape),
        ],
        out_shape=[
            jax.ShapeDtypeStruct((wide, length), BF16),
            jax.ShapeDtypeStruct((pairs, 2 * blocks, 2 * HD), F32),
            jax.ShapeDtypeStruct(bias_shape, F32),
        ],
        scratch_shapes=[pltpu.VMEM((HD, length), BF16)],
        compiler_params=params(),
        cost_estimate=LIGHT,
        name="attend",
    )(place, segs, q, k, v)


def backward_kernel(place, q, k, v, stats, bias, *rest):
    terms, (dq, dk, dv, k_t, dk_sum, dv_sum) = rest[:6], rest[6:]
    y, low = place[0], place[1]
    blocks = q.shape[0] // HD
    half = HD // 2

    @pl.when(pl.program_id(0) == 0)
    def _():
        k_t[...] = k[...].astype(F32).T.astype(BF16)
        dk_sum[...] = jnp.zeros_like(dk_sum)
        dv_sum[...] = jnp.zeros_like(dv_sum)

    for b in range(blocks):
        first, last = key_range(b)
        rows = pl.ds(pl.multiple_of(lax.rem(b - y + 4, 4) * half, half), half)
        same = terms[0][rows] + terms[1][0, rows].astype(F32) + terms[2][rows].astype(F32)
        flip = terms[3][rows] + terms[4][0, rows].astype(F32) + terms[5][rows].astype(F32)
        grad = jnp.concatenate([jnp.where(low == 0, same, flip), jnp.where(low == 0, flip, same)], axis=0).astype(BF16)
        grad = jnp.concatenate([grad[:, :HD], grad[:, HD:]], axis=0)
        q2 = two_heads(q, b)
        s = nt(k[first:last], q2) * SCALE + twice(bias[b, : last - first])
        p = jnp.exp(s - stats[0, b : b + 1]) * stats[0, blocks + b : blocks + b + 1]
        dp = nt(v[first:last], grad)
        delta = jnp.sum(p * dp, axis=0, keepdims=True)
        ds = (SCALE * p * (dp - delta)).astype(BF16)
        dv_sum[first:last] += nn(p.astype(BF16), grad)
        dk_sum[first:last] += nn(ds, q2)
        x = nn(k_t[:, first:last], ds)
        for i in range(2):
            dq[b * HD : (b + 1) * HD, i * HD : (i + 1) * HD] = x[:, i * HD : (i + 1) * HD].T.astype(BF16)

    @pl.when(pl.program_id(0) == pl.num_programs(0) - 1)
    def _():
        dk[...] = dk_sum[...].astype(BF16)
        dv[...] = dv_sum[...].astype(BF16)


def backward(place, q, k, v, stats, bias, terms):
    length, wide = q.shape
    pairs, blocks = wide // (2 * HD), length // HD
    two = pl.BlockSpec((length, 2 * HD), lambda i: (0, i))
    half = pl.BlockSpec((length // 2, 2 * HD), lambda i: (0, i))
    return pl.pallas_call(
        backward_kernel,
        grid=(pairs,),
        in_specs=[
            SMEM(),
            two,
            whole(k.shape),
            whole(v.shape),
            pl.BlockSpec((1, 2 * blocks, 2 * HD), lambda i: (i, 0, 0)),
            whole(bias.shape),
        ]
        + [half, pl.BlockSpec((1, length // 2, 2 * HD), lambda i: (0, 0, i)), half] * 2,
        out_specs=[two, whole(k.shape), whole(v.shape)],
        out_shape=[jax.ShapeDtypeStruct(x.shape, BF16) for x in (q, k, v)],
        scratch_shapes=[pltpu.VMEM((HD, length), BF16), pltpu.VMEM(k.shape, F32), pltpu.VMEM(v.shape, F32)],
        compiler_params=params(),
        cost_estimate=LIGHT,
        name="attend_grad",
    )(place, q, k, v, stats, bias, *terms)


def reader(place, refs):
    y = place[0]
    if len(refs) == 8:
        return lambda p, i, e, k: refs[p * 4 + k][e, i]
    return lambda p, i, e, k: refs[e][lax.rem(y + k, 4), p, i]


def partial_kernel(count, place, *refs):
    read = reader(place, refs[:count])
    weight, keep_near, keep_other, give, x = refs[count:]
    seq = refs[count - 1].shape[-2]
    cols = refs[count - 1].shape[-1]
    half = 4 * seq
    width = weight.shape[2] // 2

    @pl.when(pl.program_id(0) == 0)
    def _():
        for e in range(2):
            for p in range(2):
                for i in range(2):
                    for k in range(4):
                        at = (p * 2 + i) * half + k * seq
                        x[at : at + seq, e * cols : (e + 1) * cols] = read(p, i, e, k)

    w = jnp.concatenate([weight[j, :, e * width : (e + 1) * width] for e in range(2) for j in range(4)], axis=1)
    for p, keep in enumerate((keep_near, keep_other)):
        total = nt(x[p * 2 * half : (p + 1) * 2 * half], w)
        keep[...] = total[:half]
        give[p] = total[half:].astype(BF16)


def partial(place, pieces, weight):
    seq, cols = pieces[-1].shape[-2:]
    heads = weight.shape[1]
    tile = heads // 2
    out = pl.BlockSpec((4 * seq, tile), lambda i: (0, i))
    shape = jax.ShapeDtypeStruct((4 * seq, heads), F32)
    return pl.pallas_call(
        functools.partial(partial_kernel, len(pieces)),
        grid=(2,),
        in_specs=[SMEM()] + [whole(x.shape) for x in pieces] + [pl.BlockSpec((4, tile, cols // 2), lambda i: (0, i, 0))],
        out_specs=[out, out, pl.BlockSpec((2, 4 * seq, tile), lambda i: (0, 0, i))],
        out_shape=[shape, shape, jax.ShapeDtypeStruct((2, 4 * seq, heads), BF16)],
        scratch_shapes=[pltpu.VMEM((16 * seq, 2 * cols), BF16)],
        compiler_params=params(),
        cost_estimate=LIGHT,
        name="partial_grad",
    )(place, *pieces, weight)


def wgrad_kernel(place, *refs):
    same, flip, outs, (out, x) = refs[:8], refs[8], refs[9:13], refs[13:]
    seq = same[0].shape[2]
    length = 8 * seq
    y = place[0]
    for p in range(2):
        for i in range(2):
            for k in range(4):
                at = (p * 2 + i) * length + 2 * k * seq
                x[at : at + seq] = same[p * 4 + k][0, i]
                x[at + seq : at + 2 * seq] = flip[lax.rem(y + k, 4), p, i]
    tile = 256
    width = out.shape[2]
    for m in range(0, out.shape[1], tile):
        total = nn(outs[0][m : m + tile], x[:length])
        for r in range(1, 4):
            total += nn(outs[r][m : m + tile], x[r * length : (r + 1) * length])
        for k in range(2):
            out[k, m : m + tile] = total[:, k * width : (k + 1) * width].astype(BF16)


def wgrad(place, half, same, flip, outs):
    _, _, seq, cols = same[0].shape
    heads = outs[0].shape[0]
    wide = cols // 2
    return pl.pallas_call(
        wgrad_kernel,
        grid=(2,),
        in_specs=[SMEM()]
        + [pl.BlockSpec((1, 2, seq, wide), lambda i: (half, 0, 0, i))] * 8
        + [pl.BlockSpec((4, 2, 2, seq, wide), lambda i: (0, 0, 0, 0, i))]
        + [whole(outs[0].shape)] * 4,
        out_specs=pl.BlockSpec((2, heads, wide // 2), lambda i: (i, 0, 0)),
        out_shape=jax.ShapeDtypeStruct((4, heads, wide // 2), BF16),
        scratch_shapes=[pltpu.VMEM((32 * seq, wide), BF16)],
        compiler_params=params(),
        cost_estimate=LIGHT,
        name="weight_grad",
    )(place, *same, flip, *outs)


def named(name, fn, x):
    with jax.named_scope("t_" + name):
        return fn(x)


def after(x, *others):
    return lax.optimization_barrier((x, *others))[0]


def shards(query_states, key_states, value_states, segment_ids, pair_margins, upstream, out_weight):
    d = lax.axis_index("dp")
    t = lax.axis_index("tensor")
    y, low = t // 2, t % 2
    place = jnp.stack([y, low, (d // 2) % 2, d % 2]).astype(jnp.int32)
    query, key, value = query_states[0], key_states[0], value_states[0]
    heads, width = out_weight.shape
    weight = lax.all_gather(out_weight, "dp", axis=0, tiled=True, axis_index_groups=Z_GROUPS).reshape(4, heads, width)

    ids = segment_ids[0]
    partner = named("ids_pair", pair, ids)
    segs = jnp.broadcast_to(ids[:, None], (ids.shape[0], HD))
    own, to_sibling, to_across, to_diagonal = prep(place, pair_margins, segs, upstream[0])

    from_across = named("other_across", across, to_across)
    from_diagonal = named("other_diagonal", diagonal, to_diagonal)
    near = jnp.stack([own, named("near_sibling", sibling, after(to_sibling, partner))], axis=1)
    n_up, n_down = named("n_up", y_up, near), named("n_down", y_down, near)
    both = jnp.where(low == 0, jnp.stack([ids, partner]), jnp.stack([partner, ids]))
    both = after(both, near)
    ids_up = named("ids_up", y_up, both)
    ids_down = named("ids_down", y_down, both)
    ids_far = named("ids_far", lambda x: lax.ppermute(x, "tensor", by_tensor(lambda i: (i + 4) % 8)), both)
    ring = jnp.stack([both, ids_down, ids_far, ids_up] * 2).reshape(8, -1)
    ids = lax.dynamic_slice(ring, ((4 - y) % 4, 0), (4, ring.shape[1])).reshape(-1)
    whole_segs = jnp.broadcast_to(ids[:, None], (ids.shape[0], HD))

    other = jnp.stack([after(from_across, n_up, n_down, ids_up, ids_down, ids_far), from_diagonal], axis=1)
    flips = [named("pair_%d" % e, pair, jnp.stack([near[e], other[e]])) for e in range(2)]

    n, o = near, other
    n_far, o_down = named("n_far", y_up, after(n_up, n_down)), named("o_down", y_down, after(o, whole_segs))
    attn_out, stats, bias = forward(place, whole_segs, after(query, n_far, o_down), key, value)
    out_across = named("out_across", across, attn_out)
    o_up, o_far = named("o_up", y_up, after(o, n_up, n_down)), named("o_far", y_down, o_down)
    flips[0] = after(flips[0], n_far, o_down)
    flips[1] = after(flips[1], attn_out)
    flips = [lax.all_gather(x, "tensor", axis=0, axis_index_groups=Y_GROUPS) for x in flips]
    near_blocks = [n, n_down, n_far, n_up]
    other_blocks = [o, o_down, o_far, o_up]
    same = [*near_blocks, *other_blocks]

    def sums(name, pieces):
        keep_near, keep_other, give = partial(place, pieces, weight)
        given = named(name + "_sibling", sibling, give)
        total = (keep_other + given[1].astype(F32)).astype(BF16)
        return keep_near, given, named(name + "_across", across, total)

    terms_same = sums("sum_same", same)
    out_near = named("out_near", sibling, after(attn_out, o_up, o_far))
    out_other = named("out_other", sibling, after(out_across, o_up, o_far))
    outs = (attn_out, out_near, out_across, out_other)

    def sum_z(x):
        return lax.psum_scatter(
            x.reshape(4 * heads, width // 2), "dp", scatter_dimension=0, tiled=True, axis_index_groups=Z_GROUPS
        )

    first = wgrad(place, 0, same, flips[0], (*outs[:3], after(out_other, terms_same[1])))
    first_sum = sum_z(after(first, flips[1], terms_same[2]))
    terms_flip = sums("sum_flip", [flips[0], after(flips[1], first)])
    last = wgrad(place, 1, same, flips[1], (*outs[:3], after(out_other, terms_flip[1])))
    last_sum = sum_z(last)
    dq, dk, dv = backward(place, query, key, value, stats, bias, [*terms_same, *terms_flip])
    weight_grad = jnp.concatenate([first_sum, last_sum], axis=1).astype(F32)
    return (dq[None], dk[None], dv[None], weight_grad)


def solution(mesh):
    in_specs = (
        P("dp", None, "tensor"),
        P("dp", None, "tensor"),
        P("dp", None, "tensor"),
        P("dp", "tensor"),
        P("dp", None),
        P("dp", "tensor", None),
        P("tensor", "dp"),
    )
    out_specs = (
        P("dp", None, "tensor"),
        P("dp", None, "tensor"),
        P("dp", None, "tensor"),
        P("tensor", "dp"),
    )
    return jax.shard_map(shards, mesh=mesh, in_specs=in_specs, out_specs=out_specs, check_vma=False)
```

```python
import functools

import jax
import jax.numpy as jnp
from jax import lax
from jax.experimental import pallas as pl
from jax.experimental.pallas import tpu as pltpu
from jax.sharding import PartitionSpec as P

HD = 128
F32 = jnp.float32
BF16 = jnp.bfloat16
SCALE = HD ** (-0.5)
VMEM_MOST = 60 * 1024 * 1024


def by_dp(step):
    return [(i, step(i)) for i in range(16)]


def by_tensor(step):
    return [(i, step(i)) for i in range(8)]


SIBLING = by_dp(lambda i: i ^ 1)
ACROSS = by_dp(lambda i: i ^ 2)
DIAGONAL = by_dp(lambda i: i ^ 3)
PAIR = by_tensor(lambda i: i ^ 1)
Y_UP = by_tensor(lambda i: (i + 2) % 8)
Y_DOWN = by_tensor(lambda i: (i - 2) % 8)
Z_UP = by_dp(lambda i: (i + 4) % 16)
Z_DOWN = by_dp(lambda i: (i - 4) % 16)
Z_GROUPS = [[z * 4 + j for z in range(4)] for j in range(4)]
Y_GROUPS = [[y * 2 + low for y in range(4)] for low in range(2)]


def sibling(x):
    return lax.ppermute(x, "dp", SIBLING)


def across(x):
    return lax.ppermute(x, "dp", ACROSS)


def diagonal(x):
    return lax.ppermute(x, "dp", DIAGONAL)


def pair(x):
    return lax.ppermute(x, "tensor", PAIR)


def z_up(x):
    return lax.ppermute(x, "dp", Z_UP)


def z_down(x):
    return lax.ppermute(x, "dp", Z_DOWN)


def y_up(x):
    return lax.ppermute(x, "tensor", Y_UP)


def y_down(x):
    return lax.ppermute(x, "tensor", Y_DOWN)


def nn(a, b):
    return lax.dot_general(a, b, (((1,), (0,)), ((), ())), preferred_element_type=F32)


def nt(a, b):
    return lax.dot_general(a, b, (((1,), (1,)), ((), ())), preferred_element_type=F32)


def cost(us):
    return pl.CostEstimate(flops=0, bytes_accessed=int(us * 3e6), transcendentals=0)


def params():
    return pltpu.CompilerParams(vmem_limit_bytes=VMEM_MOST, dimension_semantics=("arbitrary",))


SMEM = functools.partial(pl.BlockSpec, memory_space=pltpu.SMEM)


def whole(shape):
    return pl.BlockSpec(shape, lambda i: (0,) * len(shape))


def prep_kernel(place, margins, segs, up, own, to_sibling, to_across, to_diagonal):
    h, c = place[2], place[3]
    seg = segs[...]
    margin = jnp.full(seg.shape, margins[0, 0], F32)
    for p in range(1, margins.shape[1]):
        margin = jnp.where((seg >> 1) == p, margins[0, p], margin)
    factor = jax.nn.sigmoid(-margin) * jnp.where((seg & 1) == 0, -1.0, 1.0)
    width = own.shape[2]
    factor = jnp.concatenate([factor] * (width // factor.shape[1]), axis=1)

    def put(ref, hh, cc):
        for e in range(2):
            start = pl.multiple_of((hh * 2 + cc) * 2 * width, 2 * width) + e * width
            ref[e] = (up[:, pl.ds(start, width)].astype(F32) * factor).astype(BF16)

    put(own, h, c)
    put(to_sibling, h, 1 - c)
    put(to_across, 1 - h, c)
    put(to_diagonal, 1 - h, 1 - c)


def prep(place, margins, segs, up):
    seq, model = up.shape
    width = model // 32
    shape = jax.ShapeDtypeStruct((2, seq, 4 * width), BF16)
    col = pl.BlockSpec((2, seq, width), lambda i: (0, 0, i))
    return pl.pallas_call(
        prep_kernel,
        grid=(4,),
        in_specs=[SMEM(), SMEM(), whole(segs.shape), pl.BlockSpec((seq, 8 * width), lambda i: (0, i))],
        out_specs=[col] * 4,
        out_shape=[shape] * 4,
        compiler_params=params(),
        cost_estimate=cost(3),
        name="prep",
    )(place, margins, segs, up)


def key_range(block):
    return max(0, block - 2) * HD, (block + 1) * HD


def two_heads(ref, block):
    rows = slice(block * HD, (block + 1) * HD)
    return jnp.concatenate([ref[rows, :HD], ref[rows, HD:]], axis=0)


def twice(x):
    return jnp.concatenate([x, x], axis=1)


def forward_kernel(place, segs, q, k, v, out, stats, bias, v_t):
    y, low = place[0], place[1]
    blocks = q.shape[0] // HD

    @pl.when(pl.program_id(0) == 0)
    def _():
        v_t[...] = v[...].astype(F32).T.astype(BF16)
        for b in range(blocks):
            first, last = key_range(b)
            of_query = segs[b * HD : (b + 1) * HD, :].astype(F32).T[:1]
            of_key = segs[first:last, :].astype(F32)
            shape = (last - first, HD)
            query_at = lax.broadcasted_iota(jnp.int32, shape, 1) + b * HD
            key_at = lax.broadcasted_iota(jnp.int32, shape, 0) + first
            seen = (of_key == of_query) & (key_at <= query_at)
            bias[b, : last - first] = jnp.where(seen, 0.0, -1e30)

    for b in range(blocks):
        first, last = key_range(b)
        q2 = two_heads(q, b)
        s = nt(k[first:last], q2) * SCALE + twice(bias[b, : last - first])
        highest = jnp.max(s, axis=0, keepdims=True)
        e = jnp.exp(s - highest)
        inverse = 1.0 / jnp.sum(e, axis=0, keepdims=True)
        stats[0, b : b + 1] = highest
        stats[0, blocks + b : blocks + b + 1] = inverse
        a = nn(v_t[:, first:last], (e * inverse).astype(BF16))
        at = pl.multiple_of(lax.rem(b - y + 4, 4) * HD, HD)
        for i in range(2):
            x = a[:, i * HD : (i + 1) * HD]
            x = jnp.where(low == 0, x, pltpu.roll(x, HD // 2, 1))
            out[i * HD : (i + 1) * HD, pl.ds(at, HD)] = x.astype(BF16)


def forward(place, segs, q, k, v):
    length, wide = q.shape
    pairs, blocks = wide // (2 * HD), length // HD
    bias_shape = (blocks, 3 * HD, HD)
    return pl.pallas_call(
        forward_kernel,
        grid=(pairs,),
        in_specs=[
            SMEM(),
            whole(segs.shape),
            pl.BlockSpec((length, 2 * HD), lambda i: (0, i)),
            whole(k.shape),
            whole(v.shape),
        ],
        out_specs=[
            pl.BlockSpec((2 * HD, length), lambda i: (i, 0)),
            pl.BlockSpec((1, 2 * blocks, 2 * HD), lambda i: (i, 0, 0)),
            whole(bias_shape),
        ],
        out_shape=[
            jax.ShapeDtypeStruct((wide, length), BF16),
            jax.ShapeDtypeStruct((pairs, 2 * blocks, 2 * HD), F32),
            jax.ShapeDtypeStruct(bias_shape, F32),
        ],
        scratch_shapes=[pltpu.VMEM((HD, length), BF16)],
        compiler_params=params(),
        cost_estimate=cost(9),
        name="attend",
    )(place, segs, q, k, v)


def backward_kernel(place, q, k, v, stats, bias, *rest):
    terms, (dq, dk, dv, k_t, dk_sum, dv_sum) = rest[:6], rest[6:]
    y, low = place[0], place[1]
    blocks = q.shape[0] // HD
    half = HD // 2

    @pl.when(pl.program_id(0) == 0)
    def _():
        k_t[...] = k[...].astype(F32).T.astype(BF16)
        dk_sum[...] = jnp.zeros_like(dk_sum)
        dv_sum[...] = jnp.zeros_like(dv_sum)

    for b in range(blocks):
        first, last = key_range(b)
        rows = pl.ds(pl.multiple_of(lax.rem(b - y + 4, 4) * half, half), half)
        same = terms[0][rows] + terms[1][0, rows].astype(F32) + terms[2][rows].astype(F32)
        flip = terms[3][rows] + terms[4][0, rows].astype(F32) + terms[5][rows].astype(F32)
        grad = jnp.concatenate([jnp.where(low == 0, same, flip), jnp.where(low == 0, flip, same)], axis=0).astype(BF16)
        grad = jnp.concatenate([grad[:, :HD], grad[:, HD:]], axis=0)
        q2 = two_heads(q, b)
        s = nt(k[first:last], q2) * SCALE + twice(bias[b, : last - first])
        p = jnp.exp(s - stats[0, b : b + 1]) * stats[0, blocks + b : blocks + b + 1]
        dp = nt(v[first:last], grad)
        delta = jnp.sum(p * dp, axis=0, keepdims=True)
        ds = (SCALE * p * (dp - delta)).astype(BF16)
        dv_sum[first:last] += nn(p.astype(BF16), grad)
        dk_sum[first:last] += nn(ds, q2)
        x = nn(k_t[:, first:last], ds)
        for i in range(2):
            dq[b * HD : (b + 1) * HD, i * HD : (i + 1) * HD] = x[:, i * HD : (i + 1) * HD].T.astype(BF16)

    @pl.when(pl.program_id(0) == pl.num_programs(0) - 1)
    def _():
        dk[...] = dk_sum[...].astype(BF16)
        dv[...] = dv_sum[...].astype(BF16)


def backward(place, q, k, v, stats, bias, terms):
    length, wide = q.shape
    pairs, blocks = wide // (2 * HD), length // HD
    two = pl.BlockSpec((length, 2 * HD), lambda i: (0, i))
    half = pl.BlockSpec((length // 2, 2 * HD), lambda i: (0, i))
    return pl.pallas_call(
        backward_kernel,
        grid=(pairs,),
        in_specs=[
            SMEM(),
            two,
            whole(k.shape),
            whole(v.shape),
            pl.BlockSpec((1, 2 * blocks, 2 * HD), lambda i: (i, 0, 0)),
            whole(bias.shape),
        ]
        + [half, pl.BlockSpec((1, length // 2, 2 * HD), lambda i: (0, 0, i)), half] * 2,
        out_specs=[two, whole(k.shape), whole(v.shape)],
        out_shape=[jax.ShapeDtypeStruct(x.shape, BF16) for x in (q, k, v)],
        scratch_shapes=[pltpu.VMEM((HD, length), BF16), pltpu.VMEM(k.shape, F32), pltpu.VMEM(v.shape, F32)],
        compiler_params=params(),
        cost_estimate=cost(9),
        name="attend_grad",
    )(place, q, k, v, stats, bias, *terms)


def reader(place, refs):
    y = place[0]
    if len(refs) == 8:
        return lambda p, i, e, k: refs[p * 4 + k].at[e, i]
    return lambda p, i, e, k: refs[0].at[lax.rem(y + k, 4), p, i] if e == 0 else refs[1 + k].at[p, i]


def partial_kernel(count, place, *refs):
    read = reader(place, refs[:count])
    weights, (keep_near, keep_other, give, x) = refs[count : count + 4], refs[count + 4 :]
    seq = refs[count - 1].shape[-2]
    half = 4 * seq
    width = weights[0].shape[1] // 2
    z = place[4]

    @pl.when(pl.program_id(0) == 0)
    def _():
        for e in range(2):
            for p in range(2):
                for i in range(2):
                    for k in range(4):
                        at = (p * 2 + i) * half + k * seq
                        for j in range(4):
                            col = pl.ds(pl.multiple_of(lax.rem(z + j, 4) * width, width), width)
                            x[at : at + seq, (j * 2 + e) * width : (j * 2 + e + 1) * width] = read(p, i, e, k)[:, col]

    w = jnp.concatenate([weight[...] for weight in weights], axis=1)
    for p, keep in enumerate((keep_near, keep_other)):
        total = nt(x[p * 2 * half : (p + 1) * 2 * half], w)
        keep[...] = total[:half]
        give[p] = total[half:].astype(BF16)


def partial(place, pieces, weights):
    seq, cols = pieces[-1].shape[-2:]
    heads = weights[0].shape[0]
    tile = heads // 2
    out = pl.BlockSpec((4 * seq, tile), lambda i: (0, i))
    shape = jax.ShapeDtypeStruct((4 * seq, heads), F32)
    return pl.pallas_call(
        functools.partial(partial_kernel, len(pieces)),
        grid=(2,),
        in_specs=[SMEM()] + [whole(x.shape) for x in pieces] + [pl.BlockSpec((tile, cols // 2), lambda i: (i, 0))] * 4,
        out_specs=[out, out, pl.BlockSpec((2, 4 * seq, tile), lambda i: (0, 0, i))],
        out_shape=[shape, shape, jax.ShapeDtypeStruct((2, 4 * seq, heads), BF16)],
        scratch_shapes=[pltpu.VMEM((16 * seq, 2 * cols), BF16)],
        compiler_params=params(),
        cost_estimate=cost(9),
        name="partial_grad",
    )(place, *pieces, *weights)


def wgrad_kernel(place, *refs):
    same, flip, outs, (out, x) = refs[:8], refs[8:-6], refs[-6:-2], refs[-2:]
    seq = same[0].shape[2]
    length = 8 * seq
    y = place[0]
    for p in range(2):
        for i in range(2):
            for k in range(4):
                at = (p * 2 + i) * length + 2 * k * seq
                x[at : at + seq] = same[p * 4 + k][0, i]
                x[at + seq : at + 2 * seq] = flip[k][p, i] if len(flip) > 1 else flip[0][lax.rem(y + k, 4), p, i]
    tile = 256
    width = out.shape[2]
    for m in range(0, out.shape[1], tile):
        total = nn(outs[0][m : m + tile], x[:length])
        for r in range(1, 4):
            total += nn(outs[r][m : m + tile], x[r * length : (r + 1) * length])
        for k in range(2):
            out[k, m : m + tile] = total[:, k * width : (k + 1) * width].astype(BF16)


def wgrad(place, half, same, flip, outs):
    _, _, seq, cols = same[0].shape
    heads = outs[0].shape[0]
    wide = cols // 2
    if len(flip) > 1:
        flip_spec = pl.BlockSpec((2, 2, seq, wide), lambda i: (0, 0, 0, i))
    else:
        flip_spec = pl.BlockSpec((4, 2, 2, seq, wide), lambda i: (0, 0, 0, 0, i))
    return pl.pallas_call(
        wgrad_kernel,
        grid=(2,),
        in_specs=[SMEM()]
        + [pl.BlockSpec((1, 2, seq, wide), lambda i: (half, 0, 0, i))] * 8
        + [flip_spec] * len(flip)
        + [whole(outs[0].shape)] * 4,
        out_specs=pl.BlockSpec((2, heads, wide // 2), lambda i: (i, 0, 0)),
        out_shape=jax.ShapeDtypeStruct((4, heads, wide // 2), BF16),
        scratch_shapes=[pltpu.VMEM((32 * seq, wide), BF16)],
        compiler_params=params(),
        cost_estimate=cost(9),
        name="weight_grad",
    )(place, *same, *flip, *outs)


def named(name, fn, x):
    with jax.named_scope("t_" + name):
        return fn(x)


def after(x, *others):
    return lax.optimization_barrier((x, *others))[0]


def shards(query_states, key_states, value_states, segment_ids, pair_margins, upstream, out_weight):
    d = lax.axis_index("dp")
    t = lax.axis_index("tensor")
    y, low = t // 2, t % 2
    place = jnp.stack([y, low, (d // 2) % 2, d % 2, d // 4]).astype(jnp.int32)
    query, key, value = query_states[0], key_states[0], value_states[0]
    heads, width = out_weight.shape

    ids = segment_ids[0]
    partner = named("ids_pair", pair, ids)
    segs = jnp.broadcast_to(ids[:, None], (ids.shape[0], HD))
    own, to_sibling, to_across, to_diagonal = prep(place, pair_margins, segs, upstream[0])

    from_across = named("other_across", across, to_across)
    from_diagonal = named("other_diagonal", diagonal, to_diagonal)
    near = jnp.stack([own, named("near_sibling", sibling, after(to_sibling, partner))], axis=1)
    n_up, n_down = named("n_up", y_up, near), named("n_down", y_down, near)
    both = jnp.where(low == 0, jnp.stack([ids, partner]), jnp.stack([partner, ids]))
    both = after(both, near)
    ids_up = named("ids_up", y_up, both)
    ids_down = named("ids_down", y_down, both)
    ids_far = named("ids_far", lambda x: lax.ppermute(x, "tensor", by_tensor(lambda i: (i + 4) % 8)), both)
    ring = jnp.stack([both, ids_down, ids_far, ids_up] * 2).reshape(8, -1)
    ids = lax.dynamic_slice(ring, ((4 - y) % 4, 0), (4, ring.shape[1])).reshape(-1)
    whole_segs = jnp.broadcast_to(ids[:, None], (ids.shape[0], HD))

    other = jnp.stack([after(from_across, n_up, n_down, ids_up, ids_down, ids_far), from_diagonal], axis=1)
    flips = [named("pair_%d" % e, pair, jnp.stack([near[e], other[e]])) for e in range(2)]

    w_behind, w_ahead = named("w_up", z_up, out_weight), named("w_down", z_down, out_weight)
    weights = [out_weight, w_ahead, named("w_far", z_up, w_behind), w_behind]

    n, o, q = near, other, flips[1]
    n_far, o_down = named("n_far", y_up, after(n_up, n_down)), named("o_down", y_down, after(o, whole_segs))
    first_flip = lax.all_gather(after(flips[0], n_far, o_down), "tensor", axis=0, axis_index_groups=Y_GROUPS)
    attn_out, stats, bias = forward(place, whole_segs, after(query, n_up, n_down, o), key, value)
    out_across = named("out_across", across, after(attn_out, q))
    o_up, o_far = named("o_up", y_up, after(o, n_up, n_down)), named("o_far", y_down, o_down)
    q = after(q, n_far, o_down)
    q_up, q_down = named("q_up", y_up, q), named("q_down", y_down, after(q, o_up, o_far))
    q_far = named("q_far", y_down, q_down)
    near_blocks = [n, n_down, n_far, n_up]
    other_blocks = [o, o_down, o_far, o_up]
    same = [*near_blocks, *other_blocks]

    def sums(name, pieces):
        keep_near, keep_other, give = partial(place, pieces, weights)
        given = named(name + "_sibling", sibling, give)
        total = (keep_other + given[1].astype(F32)).astype(BF16)
        return keep_near, given, named(name + "_across", across, total)

    terms_same = sums("sum_same", same)
    out_near = named("out_near", sibling, after(attn_out, o_up, o_far))
    out_other = named("out_other", sibling, after(out_across, o_up, o_far))
    outs = (attn_out, out_near, out_across, out_other)

    def sum_z(x):
        return lax.psum_scatter(
            x.reshape(4 * heads, width // 2), "dp", scatter_dimension=0, tiled=True, axis_index_groups=Z_GROUPS
        )

    flip_blocks = [q, q_down, q_far, q_up]
    first = wgrad(place, 0, same, [first_flip], (*outs[:3], after(out_other, terms_same[1], q_up, q_down)))
    first_sum = sum_z(after(first, terms_same[2], q_far))
    last = wgrad(place, 1, same, flip_blocks, (*outs[:3], after(out_other, first)))
    last_sum = sum_z(last)
    terms_flip = sums("sum_flip", [after(first_flip, last), *flip_blocks])
    dq, dk, dv = backward(place, query, key, value, stats, bias, [*terms_same, *terms_flip])
    weight_grad = jnp.concatenate([first_sum, last_sum], axis=1).astype(F32)
    return (dq[None], dk[None], dv[None], weight_grad)


def solution(mesh):
    in_specs = (
        P("dp", None, "tensor"),
        P("dp", None, "tensor"),
        P("dp", None, "tensor"),
        P("dp", "tensor"),
        P("dp", None),
        P("dp", "tensor", None),
        P("tensor", "dp"),
    )
    out_specs = (
        P("dp", None, "tensor"),
        P("dp", None, "tensor"),
        P("dp", None, "tensor"),
        P("tensor", "dp"),
    )
    return jax.shard_map(shards, mesh=mesh, in_specs=in_specs, out_specs=out_specs, check_vma=False)
```

```python
import functools

import jax
import jax.numpy as jnp
from jax import lax
from jax.experimental import pallas as pl
from jax.experimental.pallas import tpu as pltpu
from jax.sharding import PartitionSpec as P

HD = 128
F32 = jnp.float32
BF16 = jnp.bfloat16
SCALE = HD ** (-0.5)
VMEM_MOST = 60 * 1024 * 1024


def by_dp(step):
    return [(i, step(i)) for i in range(16)]


def by_tensor(step):
    return [(i, step(i)) for i in range(8)]


SIBLING = by_dp(lambda i: i ^ 1)
ACROSS = by_dp(lambda i: i ^ 2)
DIAGONAL = by_dp(lambda i: i ^ 3)
PAIR = by_tensor(lambda i: i ^ 1)
Y_UP = by_tensor(lambda i: (i + 2) % 8)
Y_DOWN = by_tensor(lambda i: (i - 2) % 8)
Z_GROUPS = [[z * 4 + j for z in range(4)] for j in range(4)]


def sibling(x):
    return lax.ppermute(x, "dp", SIBLING)


def across(x):
    return lax.ppermute(x, "dp", ACROSS)


def diagonal(x):
    return lax.ppermute(x, "dp", DIAGONAL)


def pair(x):
    return lax.ppermute(x, "tensor", PAIR)


def y_up(x):
    return lax.ppermute(x, "tensor", Y_UP)


def y_down(x):
    return lax.ppermute(x, "tensor", Y_DOWN)


def nn(a, b):
    return lax.dot_general(a, b, (((1,), (0,)), ((), ())), preferred_element_type=F32)


def nt(a, b):
    return lax.dot_general(a, b, (((1,), (1,)), ((), ())), preferred_element_type=F32)


def cost(us):
    return pl.CostEstimate(flops=0, bytes_accessed=int(us * 3e6), transcendentals=0)


def params():
    return pltpu.CompilerParams(vmem_limit_bytes=VMEM_MOST, dimension_semantics=("arbitrary",))


SMEM = functools.partial(pl.BlockSpec, memory_space=pltpu.SMEM)


def whole(shape):
    return pl.BlockSpec(shape, lambda i: (0,) * len(shape))


def prep_kernel(place, margins, segs, up, own, to_sibling, to_across, to_diagonal):
    h, c = place[2], place[3]
    seg = segs[...]
    margin = jnp.full(seg.shape, margins[0, 0], F32)
    for p in range(1, margins.shape[1]):
        margin = jnp.where((seg >> 1) == p, margins[0, p], margin)
    factor = jax.nn.sigmoid(-margin) * jnp.where((seg & 1) == 0, -1.0, 1.0)
    width = own.shape[2]
    factor = jnp.concatenate([factor] * (width // factor.shape[1]), axis=1)

    def put(ref, hh, cc):
        for e in range(2):
            start = pl.multiple_of((hh * 2 + cc) * 2 * width, 2 * width) + e * width
            ref[e] = (up[:, pl.ds(start, width)].astype(F32) * factor).astype(BF16)

    put(own, h, c)
    put(to_sibling, h, 1 - c)
    put(to_across, 1 - h, c)
    put(to_diagonal, 1 - h, 1 - c)


def prep(place, margins, segs, up):
    seq, model = up.shape
    width = model // 32
    shape = jax.ShapeDtypeStruct((2, seq, 4 * width), BF16)
    col = pl.BlockSpec((2, seq, width), lambda i: (0, 0, i))
    return pl.pallas_call(
        prep_kernel,
        grid=(4,),
        in_specs=[SMEM(), SMEM(), whole(segs.shape), pl.BlockSpec((seq, 8 * width), lambda i: (0, i))],
        out_specs=[col] * 4,
        out_shape=[shape] * 4,
        compiler_params=params(),
        cost_estimate=cost(3),
        name="prep",
    )(place, margins, segs, up)


def key_range(block):
    return max(0, block - 2) * HD, (block + 1) * HD


def two_heads(ref, block):
    rows = slice(block * HD, (block + 1) * HD)
    return jnp.concatenate([ref[rows, :HD], ref[rows, HD:]], axis=0)


def twice(x):
    return jnp.concatenate([x, x], axis=1)


def forward_kernel(place, segs, q, k, v, out, stats, bias, v_t):
    y, low = place[0], place[1]
    blocks = q.shape[0] // HD

    @pl.when(pl.program_id(0) == 0)
    def _():
        v_t[...] = v[...].astype(F32).T.astype(BF16)
        for b in range(blocks):
            first, last = key_range(b)
            of_query = segs[b * HD : (b + 1) * HD, :].astype(F32).T[:1]
            of_key = segs[first:last, :].astype(F32)
            shape = (last - first, HD)
            query_at = lax.broadcasted_iota(jnp.int32, shape, 1) + b * HD
            key_at = lax.broadcasted_iota(jnp.int32, shape, 0) + first
            seen = (of_key == of_query) & (key_at <= query_at)
            bias[b, : last - first] = jnp.where(seen, 0.0, -1e30)

    for b in range(blocks):
        first, last = key_range(b)
        q2 = two_heads(q, b)
        s = nt(k[first:last], q2) * SCALE + twice(bias[b, : last - first])
        highest = jnp.max(s, axis=0, keepdims=True)
        e = jnp.exp(s - highest)
        inverse = 1.0 / jnp.sum(e, axis=0, keepdims=True)
        stats[0, b : b + 1] = highest
        stats[0, blocks + b : blocks + b + 1] = inverse
        a = nn(v_t[:, first:last], (e * inverse).astype(BF16))
        at = pl.multiple_of(lax.rem(b - y + 4, 4) * HD, HD)
        for i in range(2):
            x = a[:, i * HD : (i + 1) * HD]
            x = jnp.where(low == 0, x, pltpu.roll(x, HD // 2, 1))
            out[i * HD : (i + 1) * HD, pl.ds(at, HD)] = x.astype(BF16)


def forward(place, segs, q, k, v):
    length, wide = q.shape
    pairs, blocks = wide // (2 * HD), length // HD
    bias_shape = (blocks, 3 * HD, HD)
    return pl.pallas_call(
        forward_kernel,
        grid=(pairs,),
        in_specs=[
            SMEM(),
            whole(segs.shape),
            pl.BlockSpec((length, 2 * HD), lambda i: (0, i)),
            whole(k.shape),
            whole(v.shape),
        ],
        out_specs=[
            pl.BlockSpec((2 * HD, length), lambda i: (i, 0)),
            pl.BlockSpec((1, 2 * blocks, 2 * HD), lambda i: (i, 0, 0)),
            whole(bias_shape),
        ],
        out_shape=[
            jax.ShapeDtypeStruct((wide, length), BF16),
            jax.ShapeDtypeStruct((pairs, 2 * blocks, 2 * HD), F32),
            jax.ShapeDtypeStruct(bias_shape, F32),
        ],
        scratch_shapes=[pltpu.VMEM((HD, length), BF16)],
        compiler_params=params(),
        cost_estimate=cost(9),
        name="attend",
    )(place, segs, q, k, v)


def backward_kernel(place, q, k, v, stats, bias, *rest):
    terms, (dq, dk, dv, k_t, dk_sum, dv_sum) = rest[:6], rest[6:]
    y, low = place[0], place[1]
    blocks = q.shape[0] // HD
    half = HD // 2

    @pl.when(pl.program_id(0) == 0)
    def _():
        k_t[...] = k[...].astype(F32).T.astype(BF16)
        dk_sum[...] = jnp.zeros_like(dk_sum)
        dv_sum[...] = jnp.zeros_like(dv_sum)

    for b in range(blocks):
        first, last = key_range(b)
        rows = pl.ds(pl.multiple_of(lax.rem(b - y + 4, 4) * half, half), half)
        same = terms[0][rows] + terms[1][0, rows].astype(F32) + terms[2][rows].astype(F32)
        flip = terms[3][rows] + terms[4][0, rows].astype(F32) + terms[5][rows].astype(F32)
        grad = jnp.concatenate([jnp.where(low == 0, same, flip), jnp.where(low == 0, flip, same)], axis=0).astype(BF16)
        grad = jnp.concatenate([grad[:, :HD], grad[:, HD:]], axis=0)
        q2 = two_heads(q, b)
        s = nt(k[first:last], q2) * SCALE + twice(bias[b, : last - first])
        p = jnp.exp(s - stats[0, b : b + 1]) * stats[0, blocks + b : blocks + b + 1]
        dp = nt(v[first:last], grad)
        delta = jnp.sum(p * dp, axis=0, keepdims=True)
        ds = (SCALE * p * (dp - delta)).astype(BF16)
        dv_sum[first:last] += nn(p.astype(BF16), grad)
        dk_sum[first:last] += nn(ds, q2)
        x = nn(k_t[:, first:last], ds)
        for i in range(2):
            dq[b * HD : (b + 1) * HD, i * HD : (i + 1) * HD] = x[:, i * HD : (i + 1) * HD].T.astype(BF16)

    @pl.when(pl.program_id(0) == pl.num_programs(0) - 1)
    def _():
        dk[...] = dk_sum[...].astype(BF16)
        dv[...] = dv_sum[...].astype(BF16)


def backward(place, q, k, v, stats, bias, terms):
    length, wide = q.shape
    pairs, blocks = wide // (2 * HD), length // HD
    two = pl.BlockSpec((length, 2 * HD), lambda i: (0, i))
    half = pl.BlockSpec((length // 2, 2 * HD), lambda i: (0, i))
    return pl.pallas_call(
        backward_kernel,
        grid=(pairs,),
        in_specs=[
            SMEM(),
            two,
            whole(k.shape),
            whole(v.shape),
            pl.BlockSpec((1, 2 * blocks, 2 * HD), lambda i: (i, 0, 0)),
            whole(bias.shape),
        ]
        + [half, pl.BlockSpec((1, length // 2, 2 * HD), lambda i: (0, 0, i)), half] * 2,
        out_specs=[two, whole(k.shape), whole(v.shape)],
        out_shape=[jax.ShapeDtypeStruct(x.shape, BF16) for x in (q, k, v)],
        scratch_shapes=[pltpu.VMEM((HD, length), BF16), pltpu.VMEM(k.shape, F32), pltpu.VMEM(v.shape, F32)],
        compiler_params=params(),
        cost_estimate=cost(9),
        name="attend_grad",
    )(place, q, k, v, stats, bias, *terms)


def partial_kernel(by_half, *refs):
    pieces, (weight, keep_near, keep_other, give, x) = refs[:8], refs[8:]
    _, _, seq, cols = pieces[0].shape
    half = 4 * seq
    width = weight.shape[2] // 2

    @pl.when(pl.program_id(0) == 0)
    def _():
        for e in range(2):
            for p in range(2):
                for i in range(2):
                    for k in range(4):
                        at = (p * 2 + i) * half + k * seq
                        piece = pieces[e * 4 + k][p, i] if by_half else pieces[p * 4 + k][e, i]
                        x[at : at + seq, e * cols : (e + 1) * cols] = piece

    w = jnp.concatenate([weight[j, :, e * width : (e + 1) * width] for e in range(2) for j in range(4)], axis=1)
    for p, keep in enumerate((keep_near, keep_other)):
        total = nt(x[p * 2 * half : (p + 1) * 2 * half], w)
        keep[...] = total[:half]
        give[p] = total[half:].astype(BF16)


def partial(by_half, pieces, weight):
    _, _, seq, cols = pieces[0].shape
    heads = weight.shape[1]
    tile = heads // 2
    out = pl.BlockSpec((4 * seq, tile), lambda i: (0, i))
    shape = jax.ShapeDtypeStruct((4 * seq, heads), F32)
    return pl.pallas_call(
        functools.partial(partial_kernel, by_half),
        grid=(2,),
        in_specs=[whole(x.shape) for x in pieces] + [pl.BlockSpec((4, tile, cols // 2), lambda i: (0, i, 0))],
        out_specs=[out, out, pl.BlockSpec((2, 4 * seq, tile), lambda i: (0, 0, i))],
        out_shape=[shape, shape, jax.ShapeDtypeStruct((2, 4 * seq, heads), BF16)],
        scratch_shapes=[pltpu.VMEM((16 * seq, 2 * cols), BF16)],
        compiler_params=params(),
        cost_estimate=cost(9),
        name="partial_grad",
    )(*pieces, weight)


def wgrad_kernel(*refs):
    same, flip, outs, (out, x) = refs[:8], refs[8:12], refs[12:16], refs[-2:]
    seq = same[0].shape[2]
    length = 8 * seq
    for p in range(2):
        for i in range(2):
            for k in range(4):
                at = (p * 2 + i) * length + 2 * k * seq
                x[at : at + seq] = same[p * 4 + k][0, i]
                x[at + seq : at + 2 * seq] = flip[k][p, i]
    tile = 256
    width = out.shape[2]
    for m in range(0, out.shape[1], tile):
        total = nn(outs[0][m : m + tile], x[:length])
        for r in range(1, 4):
            total += nn(outs[r][m : m + tile], x[r * length : (r + 1) * length])
        for k in range(2):
            out[k, m : m + tile] = total[:, k * width : (k + 1) * width].astype(BF16)


def wgrad(half, same, flip, outs, into=None):
    _, _, seq, cols = same[0].shape
    heads = outs[0].shape[0]
    wide = cols // 2
    kept = [] if into is None else [into]
    return pl.pallas_call(
        wgrad_kernel,
        grid=(2,),
        in_specs=[pl.BlockSpec((1, 2, seq, wide), lambda i: (half, 0, 0, i))] * 8
        + [pl.BlockSpec((2, 2, seq, wide), lambda i: (0, 0, 0, i))] * 4
        + [whole(outs[0].shape)] * 4
        + [pl.BlockSpec(memory_space=pl.ANY)] * len(kept),
        out_specs=pl.BlockSpec((2, heads, wide // 2), lambda i: (i, 0, half)),
        out_shape=jax.ShapeDtypeStruct((4, heads, wide), BF16),
        scratch_shapes=[pltpu.VMEM((32 * seq, wide), BF16)],
        input_output_aliases={16: 0} if kept else {},
        compiler_params=params(),
        cost_estimate=cost(9),
        name="weight_grad",
    )(*same, *flip, *outs, *kept)


def named(name, fn, x):
    with jax.named_scope("t_" + name):
        return fn(x)


def after(x, *others):
    return lax.optimization_barrier((x, *others))[0]


def shards(query_states, key_states, value_states, segment_ids, pair_margins, upstream, out_weight):
    d = lax.axis_index("dp")
    t = lax.axis_index("tensor")
    y, low = t // 2, t % 2
    place = jnp.stack([y, low, (d // 2) % 2, d % 2]).astype(jnp.int32)
    query, key, value = query_states[0], key_states[0], value_states[0]
    heads, width = out_weight.shape

    weight = lax.all_gather(out_weight, "dp", axis=0, tiled=True, axis_index_groups=Z_GROUPS).reshape(4, heads, width)
    ids = segment_ids[0]
    partner = named("ids_pair", pair, ids)
    segs = jnp.broadcast_to(ids[:, None], (ids.shape[0], HD))
    own, to_sibling, to_across, to_diagonal = prep(place, pair_margins, segs, upstream[0])

    from_across = named("other_across", across, to_across)
    from_diagonal = named("other_diagonal", diagonal, to_diagonal)
    near = jnp.stack([own, named("near_sibling", sibling, after(to_sibling, partner))], axis=1)
    n_up, n_down = named("n_up", y_up, near), named("n_down", y_down, near)
    both = jnp.where(low == 0, jnp.stack([ids, partner]), jnp.stack([partner, ids]))
    next_ids = named("ids_next", lambda x: lax.ppermute(x, "tensor", by_tensor(lambda i: i ^ 2)), after(both, near))
    half = jnp.where(y % 2 == 0, jnp.stack([both, next_ids]), jnp.stack([next_ids, both]))
    rest_ids = named("ids_rest", lambda x: lax.ppermute(x, "tensor", by_tensor(lambda i: i ^ 4)), half)
    ids = jnp.where(y < 2, jnp.stack([half, rest_ids]), jnp.stack([rest_ids, half])).reshape(-1)
    whole_segs = jnp.broadcast_to(ids[:, None], (ids.shape[0], HD))

    other = jnp.stack([after(from_across, n_up, n_down, next_ids), from_diagonal], axis=1)
    flips = [named("pair_%d" % e, pair, jnp.stack([near[e], other[e]])) for e in range(2)]

    n, o, p, q = near, other, flips[0], flips[1]
    n_far, o_down = named("n_far", y_up, n_up), named("o_down", y_down, after(o, whole_segs))
    attn_out, stats, bias = forward(place, whole_segs, after(query, n_far, o_down), key, value)
    out_across = named("out_across", across, after(attn_out, p, q))
    o_up, o_far = named("o_up", y_up, after(o, n_up, n_down)), named("o_far", y_down, o_down)
    p = after(p, n_far, o_down)
    p_up, p_down = named("p_up", y_up, p), named("p_down", y_down, p)
    p_far, q_down = named("p_far", y_up, p_up), named("q_down", y_down, after(q, o_up, o_far))
    q_up, q_far = named("q_up", y_up, after(q, p_up, p_down)), named("q_far", y_down, q_down)
    near_blocks = [n, n_down, n_far, n_up]
    other_blocks = [o, o_down, o_far, o_up]
    same = [*near_blocks, *other_blocks]

    def sums(name, by_half, pieces):
        keep_near, keep_other, give = partial(by_half, pieces, weight)
        given = named(name + "_sibling", sibling, give)
        total = (keep_other + given[1].astype(F32)).astype(BF16)
        return keep_near, given, named(name + "_across", across, total)

    terms_same = sums("sum_same", False, [after(n, p_up, p_down), *same[1:]])
    out_near = named("out_near", sibling, after(attn_out, o_up, o_far))
    out_other = named("out_other", sibling, after(out_across, o_up, o_far))
    outs = (attn_out, out_near, out_across, out_other)

    flips = [[p, p_down, p_far, p_up], [q, q_down, q_far, q_up]]
    first = wgrad(0, same, flips[0], (*outs[:3], after(out_other, terms_same[1])))
    total = wgrad(1, same, flips[1], outs, first)
    total = after(total.reshape(4 * heads, width), terms_same[2])
    weight_grad = lax.psum_scatter(total, "dp", scatter_dimension=0, tiled=True, axis_index_groups=Z_GROUPS)
    terms_flip = sums("sum_flip", True, [after(p, total), *flips[0][1:], *flips[1]])
    dq, dk, dv = backward(place, query, key, value, stats, bias, [*terms_same, *terms_flip])
    return (dq[None], dk[None], dv[None], weight_grad.astype(F32))


def solution(mesh):
    in_specs = (
        P("dp", None, "tensor"),
        P("dp", None, "tensor"),
        P("dp", None, "tensor"),
        P("dp", "tensor"),
        P("dp", None),
        P("dp", "tensor", None),
        P("tensor", "dp"),
    )
    out_specs = (
        P("dp", None, "tensor"),
        P("dp", None, "tensor"),
        P("dp", None, "tensor"),
        P("tensor", "dp"),
    )
    return jax.shard_map(shards, mesh=mesh, in_specs=in_specs, out_specs=out_specs, check_vma=False)
```

```python
import functools

import jax
import jax.numpy as jnp
from jax import lax
from jax.experimental import pallas as pl
from jax.experimental.pallas import tpu as pltpu
from jax.sharding import PartitionSpec as P

HD = 128
F32 = jnp.float32
BF16 = jnp.bfloat16
SCALE = HD ** (-0.5)
VMEM_MOST = 60 * 1024 * 1024


def by_dp(step):
    return [(i, step(i)) for i in range(16)]


def by_tensor(step):
    return [(i, step(i)) for i in range(8)]


SIBLING = by_dp(lambda i: i ^ 1)
ACROSS = by_dp(lambda i: i ^ 2)
DIAGONAL = by_dp(lambda i: i ^ 3)
PAIR = by_tensor(lambda i: i ^ 1)
Y_UP = by_tensor(lambda i: (i + 2) % 8)
Y_DOWN = by_tensor(lambda i: (i - 2) % 8)
Z_GROUPS = [[z * 4 + j for z in range(4)] for j in range(4)]


def sibling(x):
    return lax.ppermute(x, "dp", SIBLING)


def across(x):
    return lax.ppermute(x, "dp", ACROSS)


def diagonal(x):
    return lax.ppermute(x, "dp", DIAGONAL)


def pair(x):
    return lax.ppermute(x, "tensor", PAIR)


def y_up(x):
    return lax.ppermute(x, "tensor", Y_UP)


def y_down(x):
    return lax.ppermute(x, "tensor", Y_DOWN)


def nn(a, b):
    return lax.dot_general(a, b, (((1,), (0,)), ((), ())), preferred_element_type=F32)


def nt(a, b):
    return lax.dot_general(a, b, (((1,), (1,)), ((), ())), preferred_element_type=F32)


def cost(us):
    return pl.CostEstimate(flops=0, bytes_accessed=int(us * 3e6), transcendentals=0)


def params():
    return pltpu.CompilerParams(vmem_limit_bytes=VMEM_MOST, dimension_semantics=("arbitrary",))


SMEM = functools.partial(pl.BlockSpec, memory_space=pltpu.SMEM)


def whole(shape):
    return pl.BlockSpec(shape, lambda i: (0,) * len(shape))


def prep_kernel(place, margins, segs, up, own, to_sibling, to_across, to_diagonal):
    h, c = place[2], place[3]
    seg = segs[...]
    margin = jnp.full(seg.shape, margins[0, 0], F32)
    for p in range(1, margins.shape[1]):
        margin = jnp.where((seg >> 1) == p, margins[0, p], margin)
    factor = jax.nn.sigmoid(-margin) * jnp.where((seg & 1) == 0, -1.0, 1.0)
    width = own.shape[2]
    factor = jnp.concatenate([factor] * (width // factor.shape[1]), axis=1)

    def put(ref, hh, cc):
        for e in range(2):
            start = pl.multiple_of((hh * 2 + cc) * 2 * width, 2 * width) + e * width
            ref[e] = (up[:, pl.ds(start, width)].astype(F32) * factor).astype(BF16)

    put(own, h, c)
    put(to_sibling, h, 1 - c)
    put(to_across, 1 - h, c)
    put(to_diagonal, 1 - h, 1 - c)


def prep(place, margins, segs, up):
    seq, model = up.shape
    width = model // 32
    shape = jax.ShapeDtypeStruct((2, seq, 4 * width), BF16)
    col = pl.BlockSpec((2, seq, width), lambda i: (0, 0, i))
    return pl.pallas_call(
        prep_kernel,
        grid=(4,),
        in_specs=[SMEM(), SMEM(), whole(segs.shape), pl.BlockSpec((seq, 8 * width), lambda i: (0, i))],
        out_specs=[col] * 4,
        out_shape=[shape] * 4,
        compiler_params=params(),
        cost_estimate=cost(3),
        name="prep",
    )(place, margins, segs, up)


def key_range(block):
    return max(0, block - 2) * HD, (block + 1) * HD


def two_heads(ref, block):
    rows = slice(block * HD, (block + 1) * HD)
    return jnp.concatenate([ref[rows, :HD], ref[rows, HD:]], axis=0)


def twice(x):
    return jnp.concatenate([x, x], axis=1)


def forward_kernel(place, segs, q, k, v, out, stats, bias, v_t):
    y, low = place[0], place[1]
    blocks = q.shape[0] // HD

    @pl.when(pl.program_id(0) == 0)
    def _():
        v_t[...] = v[...].astype(F32).T.astype(BF16)
        for b in range(blocks):
            first, last = key_range(b)
            of_query = segs[b * HD : (b + 1) * HD, :].astype(F32).T[:1]
            of_key = segs[first:last, :].astype(F32)
            shape = (last - first, HD)
            query_at = lax.broadcasted_iota(jnp.int32, shape, 1) + b * HD
            key_at = lax.broadcasted_iota(jnp.int32, shape, 0) + first
            seen = (of_key == of_query) & (key_at <= query_at)
            bias[b, : last - first] = jnp.where(seen, 0.0, -1e30)

    for b in range(blocks):
        first, last = key_range(b)
        q2 = two_heads(q, b)
        s = nt(k[first:last], q2) * SCALE + twice(bias[b, : last - first])
        highest = jnp.max(s, axis=0, keepdims=True)
        e = jnp.exp(s - highest)
        inverse = 1.0 / jnp.sum(e, axis=0, keepdims=True)
        stats[0, b : b + 1] = highest
        stats[0, blocks + b : blocks + b + 1] = inverse
        a = nn(v_t[:, first:last], (e * inverse).astype(BF16))
        at = pl.multiple_of(lax.rem(b - y + 4, 4) * HD, HD)
        for i in range(2):
            x = a[:, i * HD : (i + 1) * HD]
            x = jnp.where(low == 0, x, pltpu.roll(x, HD // 2, 1))
            out[i * HD : (i + 1) * HD, pl.ds(at, HD)] = x.astype(BF16)


def forward(place, segs, q, k, v):
    length, wide = q.shape
    pairs, blocks = wide // (2 * HD), length // HD
    bias_shape = (blocks, 3 * HD, HD)
    return pl.pallas_call(
        forward_kernel,
        grid=(pairs,),
        in_specs=[
            SMEM(),
            whole(segs.shape),
            pl.BlockSpec((length, 2 * HD), lambda i: (0, i)),
            whole(k.shape),
            whole(v.shape),
        ],
        out_specs=[
            pl.BlockSpec((2 * HD, length), lambda i: (i, 0)),
            pl.BlockSpec((1, 2 * blocks, 2 * HD), lambda i: (i, 0, 0)),
            whole(bias_shape),
        ],
        out_shape=[
            jax.ShapeDtypeStruct((wide, length), BF16),
            jax.ShapeDtypeStruct((pairs, 2 * blocks, 2 * HD), F32),
            jax.ShapeDtypeStruct(bias_shape, F32),
        ],
        scratch_shapes=[pltpu.VMEM((HD, length), BF16)],
        compiler_params=params(),
        cost_estimate=cost(9),
        name="attend",
    )(place, segs, q, k, v)


def backward_kernel(place, q, k, v, stats, bias, *rest):
    terms, (dq, dk, dv, k_t, dk_sum, dv_sum) = rest[:6], rest[6:]
    y, low = place[0], place[1]
    blocks = q.shape[0] // HD
    half = HD // 2

    @pl.when(pl.program_id(0) == 0)
    def _():
        k_t[...] = k[...].astype(F32).T.astype(BF16)
        dk_sum[...] = jnp.zeros_like(dk_sum)
        dv_sum[...] = jnp.zeros_like(dv_sum)

    for b in range(blocks):
        first, last = key_range(b)
        rows = pl.ds(pl.multiple_of(lax.rem(b - y + 4, 4) * half, half), half)
        same = terms[0][rows] + terms[1][0, rows].astype(F32) + terms[2][rows].astype(F32)
        flip = terms[3][rows] + terms[4][0, rows].astype(F32) + terms[5][rows].astype(F32)
        grad = jnp.concatenate([jnp.where(low == 0, same, flip), jnp.where(low == 0, flip, same)], axis=0).astype(BF16)
        grad = jnp.concatenate([grad[:, :HD], grad[:, HD:]], axis=0)
        q2 = two_heads(q, b)
        s = nt(k[first:last], q2) * SCALE + twice(bias[b, : last - first])
        p = jnp.exp(s - stats[0, b : b + 1]) * stats[0, blocks + b : blocks + b + 1]
        dp = nt(v[first:last], grad)
        delta = jnp.sum(p * dp, axis=0, keepdims=True)
        ds = (SCALE * p * (dp - delta)).astype(BF16)
        dv_sum[first:last] += nn(p.astype(BF16), grad)
        dk_sum[first:last] += nn(ds, q2)
        x = nn(k_t[:, first:last], ds)
        for i in range(2):
            dq[b * HD : (b + 1) * HD, i * HD : (i + 1) * HD] = x[:, i * HD : (i + 1) * HD].T.astype(BF16)

    @pl.when(pl.program_id(0) == pl.num_programs(0) - 1)
    def _():
        dk[...] = dk_sum[...].astype(BF16)
        dv[...] = dv_sum[...].astype(BF16)


def backward(place, q, k, v, stats, bias, terms):
    length, wide = q.shape
    pairs, blocks = wide // (2 * HD), length // HD
    two = pl.BlockSpec((length, 2 * HD), lambda i: (0, i))
    half = pl.BlockSpec((length // 2, 2 * HD), lambda i: (0, i))
    return pl.pallas_call(
        backward_kernel,
        grid=(pairs,),
        in_specs=[
            SMEM(),
            two,
            whole(k.shape),
            whole(v.shape),
            pl.BlockSpec((1, 2 * blocks, 2 * HD), lambda i: (i, 0, 0)),
            whole(bias.shape),
        ]
        + [half, pl.BlockSpec((1, length // 2, 2 * HD), lambda i: (0, 0, i)), half] * 2,
        out_specs=[two, whole(k.shape), whole(v.shape)],
        out_shape=[jax.ShapeDtypeStruct(x.shape, BF16) for x in (q, k, v)],
        scratch_shapes=[pltpu.VMEM((HD, length), BF16), pltpu.VMEM(k.shape, F32), pltpu.VMEM(v.shape, F32)],
        compiler_params=params(),
        cost_estimate=cost(9),
        name="attend_grad",
    )(place, q, k, v, stats, bias, *terms)


def partial_kernel(by_half, *refs):
    pieces, (weight, keep_near, keep_other, give, x) = refs[:8], refs[8:]
    _, _, seq, cols = pieces[0].shape
    half = 4 * seq
    width = weight.shape[2] // 2

    @pl.when(pl.program_id(0) == 0)
    def _():
        for e in range(2):
            for p in range(2):
                for i in range(2):
                    for k in range(4):
                        at = (p * 2 + i) * half + k * seq
                        piece = pieces[e * 4 + k][p, i] if by_half else pieces[p * 4 + k][e, i]
                        x[at : at + seq, e * cols : (e + 1) * cols] = piece

    w = jnp.concatenate([weight[j, :, e * width : (e + 1) * width] for e in range(2) for j in range(4)], axis=1)
    for p, keep in enumerate((keep_near, keep_other)):
        total = nt(x[p * 2 * half : (p + 1) * 2 * half], w)
        keep[...] = total[:half]
        give[p] = total[half:].astype(BF16)


def partial(by_half, pieces, weight):
    _, _, seq, cols = pieces[0].shape
    heads = weight.shape[1]
    tile = heads // 2
    out = pl.BlockSpec((4 * seq, tile), lambda i: (0, i))
    shape = jax.ShapeDtypeStruct((4 * seq, heads), F32)
    return pl.pallas_call(
        functools.partial(partial_kernel, by_half),
        grid=(2,),
        in_specs=[whole(x.shape) for x in pieces] + [pl.BlockSpec((4, tile, cols // 2), lambda i: (0, i, 0))],
        out_specs=[out, out, pl.BlockSpec((2, 4 * seq, tile), lambda i: (0, 0, i))],
        out_shape=[shape, shape, jax.ShapeDtypeStruct((2, 4 * seq, heads), BF16)],
        scratch_shapes=[pltpu.VMEM((16 * seq, 2 * cols), BF16)],
        compiler_params=params(),
        cost_estimate=cost(9),
        name="partial_grad",
    )(*pieces, weight)


def wgrad_kernel(*refs):
    same, flip, outs, (out, x) = refs[:8], refs[8:12], refs[12:16], refs[-2:]
    seq = same[0].shape[2]
    length = 8 * seq
    for p in range(2):
        for i in range(2):
            for k in range(4):
                at = (p * 2 + i) * length + 2 * k * seq
                x[at : at + seq] = same[p * 4 + k][0, i]
                x[at + seq : at + 2 * seq] = flip[k][p, i]
    tile = 256
    width = out.shape[2]
    for m in range(0, out.shape[1], tile):
        total = nn(outs[0][m : m + tile], x[:length])
        for r in range(1, 4):
            total += nn(outs[r][m : m + tile], x[r * length : (r + 1) * length])
        for k in range(2):
            out[k, m : m + tile] = total[:, k * width : (k + 1) * width].astype(BF16)


def wgrad(half, same, flip, outs, into=None):
    _, _, seq, cols = same[0].shape
    heads = outs[0].shape[0]
    wide = cols // 2
    kept = [] if into is None else [into]
    return pl.pallas_call(
        wgrad_kernel,
        grid=(2,),
        in_specs=[pl.BlockSpec((1, 2, seq, wide), lambda i: (half, 0, 0, i))] * 8
        + [pl.BlockSpec((2, 2, seq, wide), lambda i: (0, 0, 0, i))] * 4
        + [whole(outs[0].shape)] * 4
        + [pl.BlockSpec(memory_space=pl.ANY)] * len(kept),
        out_specs=pl.BlockSpec((2, heads, wide // 2), lambda i: (i, 0, half)),
        out_shape=jax.ShapeDtypeStruct((4, heads, wide), BF16),
        scratch_shapes=[pltpu.VMEM((32 * seq, wide), BF16)],
        input_output_aliases={16: 0} if kept else {},
        compiler_params=params(),
        cost_estimate=cost(9),
        name="weight_grad",
    )(*same, *flip, *outs, *kept)


def named(name, fn, x):
    with jax.named_scope("t_" + name):
        return fn(x)


def after(x, *others):
    return lax.optimization_barrier((x, *others))[0]


def shards(query_states, key_states, value_states, segment_ids, pair_margins, upstream, out_weight):
    d = lax.axis_index("dp")
    t = lax.axis_index("tensor")
    y, low = t // 2, t % 2
    place = jnp.stack([y, low, (d // 2) % 2, d % 2]).astype(jnp.int32)
    query, key, value = query_states[0], key_states[0], value_states[0]
    heads, width = out_weight.shape

    weight = lax.all_gather(out_weight, "dp", axis=0, tiled=True, axis_index_groups=Z_GROUPS).reshape(4, heads, width)
    ids = segment_ids[0]
    partner = named("ids_pair", pair, ids)
    segs = jnp.broadcast_to(ids[:, None], (ids.shape[0], HD))
    own, to_sibling, to_across, to_diagonal = prep(place, pair_margins, segs, upstream[0])

    from_across = named("other_across", across, to_across)
    from_diagonal = named("other_diagonal", diagonal, to_diagonal)
    both = jnp.where(low == 0, jnp.stack([ids, partner]), jnp.stack([partner, ids]))
    next_ids = named("ids_next", lambda x: lax.ppermute(x, "tensor", by_tensor(lambda i: i ^ 2)), both)
    half = jnp.where(y % 2 == 0, jnp.stack([both, next_ids]), jnp.stack([next_ids, both]))
    rest_ids = named("ids_rest", lambda x: lax.ppermute(x, "tensor", by_tensor(lambda i: i ^ 4)), half)
    ids = jnp.where(y < 2, jnp.stack([half, rest_ids]), jnp.stack([rest_ids, half])).reshape(-1)
    whole_segs = jnp.broadcast_to(ids[:, None], (ids.shape[0], HD))

    from_sibling = named("near_sibling", sibling, after(to_sibling, partner))
    near = jnp.stack([own, after(from_sibling, rest_ids)], axis=1)
    n_up, n_down = named("n_up", y_up, near), named("n_down", y_down, near)
    attn_out, stats, bias = forward(place, whole_segs, query, key, value)
    other = jnp.stack([after(from_across, n_up, n_down, attn_out), from_diagonal], axis=1)
    flips = [named("pair_%d" % e, pair, jnp.stack([near[e], other[e]])) for e in range(2)]

    n, o, p, q = near, other, flips[0], flips[1]
    n_far, o_down = named("n_far", y_up, n_up), named("o_down", y_down, o)
    o_up, o_far = named("o_up", y_up, o), named("o_far", y_down, o_down)
    out_across = named("out_across", across, after(attn_out, p))
    p, q = after(p, n_far, o_down), after(q, o_up, o_far)
    p_up, p_down = named("p_up", y_up, p), named("p_down", y_down, p)
    p_far, q_down = named("p_far", y_up, p_up), named("q_down", y_down, q)
    q_up, q_far = named("q_up", y_up, q), named("q_far", y_down, q_down)
    near_blocks = [n, n_down, n_far, n_up]
    other_blocks = [o, o_down, o_far, o_up]
    same = [*near_blocks, *other_blocks]

    def sums(name, by_half, pieces):
        keep_near, keep_other, give = partial(by_half, pieces, weight)
        given = named(name + "_sibling", sibling, give)
        total = (keep_other + given[1].astype(F32)).astype(BF16)
        return keep_near, given, named(name + "_across", across, total)

    out_near = named("out_near", sibling, after(attn_out, o_up, o_far))
    out_other = named("out_other", sibling, after(out_across, o_up, o_far))
    outs = (attn_out, out_near, out_across, out_other)

    flips = [[p, p_down, p_far, p_up], [q, q_down, q_far, q_up]]
    first = wgrad(0, same, flips[0], outs)
    total = wgrad(1, same, flips[1], outs, first).reshape(4 * heads, width)
    weight_grad = lax.psum_scatter(total, "dp", scatter_dimension=0, tiled=True, axis_index_groups=Z_GROUPS)
    terms_same = sums("sum_same", False, [after(n, total), *same[1:]])
    terms_flip = sums("sum_flip", True, [after(p, terms_same[0]), *flips[0][1:], *flips[1]])
    dq, dk, dv = backward(place, query, key, value, stats, bias, [*terms_same, *terms_flip])
    return (dq[None], dk[None], dv[None], weight_grad.astype(F32))


def solution(mesh):
    in_specs = (
        P("dp", None, "tensor"),
        P("dp", None, "tensor"),
        P("dp", None, "tensor"),
        P("dp", "tensor"),
        P("dp", None),
        P("dp", "tensor", None),
        P("tensor", "dp"),
    )
    out_specs = (
        P("dp", None, "tensor"),
        P("dp", None, "tensor"),
        P("dp", None, "tensor"),
        P("tensor", "dp"),
    )
    return jax.shard_map(shards, mesh=mesh, in_specs=in_specs, out_specs=out_specs, check_vma=False)
```

```python
import functools

import jax
import jax.numpy as jnp
from jax import lax
from jax.experimental import pallas as pl
from jax.experimental.pallas import tpu as pltpu
from jax.sharding import PartitionSpec as P

HD = 128
F32 = jnp.float32
BF16 = jnp.bfloat16
SCALE = HD ** (-0.5)
VMEM_MOST = 60 * 1024 * 1024


def by_dp(step):
    return [(i, step(i)) for i in range(16)]


def by_tensor(step):
    return [(i, step(i)) for i in range(8)]


SIBLING = by_dp(lambda i: i ^ 1)
ACROSS = by_dp(lambda i: i ^ 2)
DIAGONAL = by_dp(lambda i: i ^ 3)
PAIR = by_tensor(lambda i: i ^ 1)
Y_UP = by_tensor(lambda i: (i + 2) % 8)
Y_DOWN = by_tensor(lambda i: (i - 2) % 8)
Z_GROUPS = [[z * 4 + j for z in range(4)] for j in range(4)]


def sibling(x):
    return lax.ppermute(x, "dp", SIBLING)


def across(x):
    return lax.ppermute(x, "dp", ACROSS)


def diagonal(x):
    return lax.ppermute(x, "dp", DIAGONAL)


def pair(x):
    return lax.ppermute(x, "tensor", PAIR)


def y_up(x):
    return lax.ppermute(x, "tensor", Y_UP)


def y_down(x):
    return lax.ppermute(x, "tensor", Y_DOWN)


def nn(a, b):
    return lax.dot_general(a, b, (((1,), (0,)), ((), ())), preferred_element_type=F32)


def nt(a, b):
    return lax.dot_general(a, b, (((1,), (1,)), ((), ())), preferred_element_type=F32)


def cost(us):
    return pl.CostEstimate(flops=0, bytes_accessed=int(us * 3e6), transcendentals=0)


def params():
    return pltpu.CompilerParams(vmem_limit_bytes=VMEM_MOST, dimension_semantics=("arbitrary",))


SMEM = functools.partial(pl.BlockSpec, memory_space=pltpu.SMEM)


def whole(shape):
    return pl.BlockSpec(shape, lambda i: (0,) * len(shape))


def prep_kernel(place, margins, segs, up, own, to_sibling, to_across, to_diagonal):
    h, c = place[2], place[3]
    seg = segs[...]
    margin = jnp.full(seg.shape, margins[0, 0], F32)
    for p in range(1, margins.shape[1]):
        margin = jnp.where((seg >> 1) == p, margins[0, p], margin)
    factor = jax.nn.sigmoid(-margin) * jnp.where((seg & 1) == 0, -1.0, 1.0)
    width = own.shape[1]
    factor = jnp.concatenate([factor] * (width // factor.shape[1]), axis=1)

    def grad(hh, cc):
        start = pl.multiple_of((hh * 2 + cc) * width, width)
        return (up[:, pl.ds(start, width)].astype(F32) * factor).astype(BF16)

    own[...] = grad(h, c)
    to_sibling[...] = grad(h, 1 - c)
    to_across[...] = grad(1 - h, c)
    to_diagonal[...] = grad(1 - h, 1 - c)


def prep(place, margins, segs, up):
    seq, model = up.shape
    width = model // 16
    col = pl.BlockSpec((seq, width), lambda i: (0, i))
    return pl.pallas_call(
        prep_kernel,
        grid=(4,),
        in_specs=[SMEM(), SMEM(), whole(segs.shape), pl.BlockSpec((seq, 4 * width), lambda i: (0, i))],
        out_specs=[col] * 4,
        out_shape=[jax.ShapeDtypeStruct((seq, 4 * width), BF16)] * 4,
        compiler_params=params(),
        cost_estimate=cost(3),
        name="prep",
    )(place, margins, segs, up)


def key_range(block):
    return max(0, block - 2) * HD, (block + 1) * HD


def two_heads(ref, block):
    rows = slice(block * HD, (block + 1) * HD)
    return jnp.concatenate([ref[rows, :HD], ref[rows, HD:]], axis=0)


def twice(x):
    return jnp.concatenate([x, x], axis=1)


def forward_kernel(place, segs, q, k, v, out, stats, bias, v_t):
    y, low = place[0], place[1]
    blocks = q.shape[0] // HD

    @pl.when(pl.program_id(0) == 0)
    def _():
        v_t[...] = v[...].astype(F32).T.astype(BF16)
        for b in range(blocks):
            first, last = key_range(b)
            of_query = segs[b * HD : (b + 1) * HD, :].astype(F32).T[:1]
            of_key = segs[first:last, :].astype(F32)
            shape = (last - first, HD)
            query_at = lax.broadcasted_iota(jnp.int32, shape, 1) + b * HD
            key_at = lax.broadcasted_iota(jnp.int32, shape, 0) + first
            seen = (of_key == of_query) & (key_at <= query_at)
            bias[b, : last - first] = jnp.where(seen, 0.0, -1e30)

    for b in range(blocks):
        first, last = key_range(b)
        q2 = two_heads(q, b)
        s = nt(k[first:last], q2) * SCALE + twice(bias[b, : last - first])
        highest = jnp.max(s, axis=0, keepdims=True)
        e = jnp.exp(s - highest)
        inverse = 1.0 / jnp.sum(e, axis=0, keepdims=True)
        stats[0, b : b + 1] = highest
        stats[0, blocks + b : blocks + b + 1] = inverse
        a = nn(v_t[:, first:last], (e * inverse).astype(BF16))
        at = pl.multiple_of(lax.rem(b - y + 4, 4) * HD, HD)
        for i in range(2):
            x = a[:, i * HD : (i + 1) * HD]
            x = jnp.where(low == 0, x, pltpu.roll(x, HD // 2, 1))
            out[i * HD : (i + 1) * HD, pl.ds(at, HD)] = x.astype(BF16)


def forward(place, segs, q, k, v):
    length, wide = q.shape
    pairs, blocks = wide // (2 * HD), length // HD
    bias_shape = (blocks, 3 * HD, HD)
    return pl.pallas_call(
        forward_kernel,
        grid=(pairs,),
        in_specs=[
            SMEM(),
            whole(segs.shape),
            pl.BlockSpec((length, 2 * HD), lambda i: (0, i)),
            whole(k.shape),
            whole(v.shape),
        ],
        out_specs=[
            pl.BlockSpec((2 * HD, length), lambda i: (i, 0)),
            pl.BlockSpec((1, 2 * blocks, 2 * HD), lambda i: (i, 0, 0)),
            whole(bias_shape),
        ],
        out_shape=[
            jax.ShapeDtypeStruct((wide, length), BF16),
            jax.ShapeDtypeStruct((pairs, 2 * blocks, 2 * HD), F32),
            jax.ShapeDtypeStruct(bias_shape, F32),
        ],
        scratch_shapes=[pltpu.VMEM((HD, length), BF16)],
        compiler_params=params(),
        cost_estimate=cost(9),
        name="attend",
    )(place, segs, q, k, v)


def backward_kernel(place, q, k, v, stats, bias, *rest):
    terms, (dq, dk, dv, k_t, dk_sum, dv_sum) = rest[:6], rest[6:]
    y, low = place[0], place[1]
    blocks = q.shape[0] // HD
    half = HD // 2

    @pl.when(pl.program_id(0) == 0)
    def _():
        k_t[...] = k[...].astype(F32).T.astype(BF16)
        dk_sum[...] = jnp.zeros_like(dk_sum)
        dv_sum[...] = jnp.zeros_like(dv_sum)

    for b in range(blocks):
        first, last = key_range(b)
        rows = pl.ds(pl.multiple_of(lax.rem(b - y + 4, 4) * half, half), half)
        same = terms[0][rows] + terms[1][0, rows].astype(F32) + terms[2][rows].astype(F32)
        flip = terms[3][rows] + terms[4][0, rows].astype(F32) + terms[5][rows].astype(F32)
        grad = jnp.concatenate([jnp.where(low == 0, same, flip), jnp.where(low == 0, flip, same)], axis=0).astype(BF16)
        grad = jnp.concatenate([grad[:, :HD], grad[:, HD:]], axis=0)
        q2 = two_heads(q, b)
        s = nt(k[first:last], q2) * SCALE + twice(bias[b, : last - first])
        p = jnp.exp(s - stats[0, b : b + 1]) * stats[0, blocks + b : blocks + b + 1]
        dp = nt(v[first:last], grad)
        delta = jnp.sum(p * dp, axis=0, keepdims=True)
        ds = (SCALE * p * (dp - delta)).astype(BF16)
        dv_sum[first:last] += nn(p.astype(BF16), grad)
        dk_sum[first:last] += nn(ds, q2)
        x = nn(k_t[:, first:last], ds)
        for i in range(2):
            dq[b * HD : (b + 1) * HD, i * HD : (i + 1) * HD] = x[:, i * HD : (i + 1) * HD].T.astype(BF16)

    @pl.when(pl.program_id(0) == pl.num_programs(0) - 1)
    def _():
        dk[...] = dk_sum[...].astype(BF16)
        dv[...] = dv_sum[...].astype(BF16)


def backward(place, q, k, v, stats, bias, terms):
    length, wide = q.shape
    pairs, blocks = wide // (2 * HD), length // HD
    two = pl.BlockSpec((length, 2 * HD), lambda i: (0, i))
    half = pl.BlockSpec((length // 2, 2 * HD), lambda i: (0, i))
    return pl.pallas_call(
        backward_kernel,
        grid=(pairs,),
        in_specs=[
            SMEM(),
            two,
            whole(k.shape),
            whole(v.shape),
            pl.BlockSpec((1, 2 * blocks, 2 * HD), lambda i: (i, 0, 0)),
            whole(bias.shape),
        ]
        + [half, pl.BlockSpec((1, length // 2, 2 * HD), lambda i: (0, 0, i)), half] * 2,
        out_specs=[two, whole(k.shape), whole(v.shape)],
        out_shape=[jax.ShapeDtypeStruct(x.shape, BF16) for x in (q, k, v)],
        scratch_shapes=[pltpu.VMEM((HD, length), BF16), pltpu.VMEM(k.shape, F32), pltpu.VMEM(v.shape, F32)],
        compiler_params=params(),
        cost_estimate=cost(9),
        name="attend_grad",
    )(place, q, k, v, stats, bias, *terms)


def partial_kernel(*refs):
    pieces, (weight, keep_near, keep_other, give, x) = refs[:8], refs[8:]
    seq = pieces[0].shape[2]
    half = 4 * seq

    @pl.when(pl.program_id(0) == 0)
    def _():
        for p in range(2):
            for i in range(2):
                for k in range(4):
                    at = (p * 2 + i) * half + k * seq
                    x[at : at + seq] = pieces[p * 4 + k][0, i]

    w = jnp.concatenate([weight[j] for j in range(4)], axis=1)
    for p, keep in enumerate((keep_near, keep_other)):
        total = nt(x[p * 2 * half : (p + 1) * 2 * half], w)
        keep[...] = total[:half]
        give[p] = total[half:].astype(BF16)


def partial(pieces, weight):
    _, _, seq, cols = pieces[0][0].shape
    heads = weight.shape[1]
    tile = heads // 2
    out = pl.BlockSpec((4 * seq, tile), lambda i: (0, i))
    shape = jax.ShapeDtypeStruct((4 * seq, heads), F32)

    def spec(index):
        return pl.BlockSpec((1, 2, seq, cols), lambda i: (index, 0, 0, 0))

    return pl.pallas_call(
        partial_kernel,
        grid=(2,),
        in_specs=[spec(index) for _, index in pieces] + [pl.BlockSpec((4, tile, cols // 4), lambda i: (0, i, 0))],
        out_specs=[out, out, pl.BlockSpec((2, 4 * seq, tile), lambda i: (0, 0, i))],
        out_shape=[shape, shape, jax.ShapeDtypeStruct((2, 4 * seq, heads), BF16)],
        scratch_shapes=[pltpu.VMEM((16 * seq, cols), BF16)],
        compiler_params=params(),
        cost_estimate=cost(9),
        name="partial_grad",
    )(*[x for x, _ in pieces], weight)


def wgrad_kernel(*refs):
    same, flip, outs, (out, x) = refs[:8], refs[8:16], refs[16:20], refs[20:]
    seq = same[0].shape[2]
    length = 8 * seq
    for p in range(2):
        for i in range(2):
            for k in range(4):
                at = (p * 2 + i) * length + 2 * k * seq
                x[at : at + seq] = same[p * 4 + k][0, i]
                x[at + seq : at + 2 * seq] = flip[p * 4 + k][0, i]
    tile = 256
    for m in range(0, out.shape[1], tile):
        total = nn(outs[0][m : m + tile], x[:length])
        for r in range(1, 4):
            total += nn(outs[r][m : m + tile], x[r * length : (r + 1) * length])
        out[0, m : m + tile] = total.astype(BF16)


def wgrad(same, flip, outs):
    _, _, seq, cols = same[0][0].shape
    heads = outs[0].shape[0]
    width = cols // 4

    def spec(index):
        return pl.BlockSpec((1, 2, seq, width), lambda i: (index, 0, 0, i))

    return pl.pallas_call(
        wgrad_kernel,
        grid=(4,),
        in_specs=[spec(index) for _, index in same + flip] + [whole(outs[0].shape)] * 4,
        out_specs=pl.BlockSpec((1, heads, width), lambda i: (i, 0, 0)),
        out_shape=jax.ShapeDtypeStruct((4, heads, width), BF16),
        scratch_shapes=[pltpu.VMEM((32 * seq, width), BF16)],
        compiler_params=params(),
        cost_estimate=cost(16),
        name="weight_grad",
    )(*[x for x, _ in same + flip], *outs)


def named(name, fn, x):
    with jax.named_scope("t_" + name):
        return fn(x)


def after(x, *others):
    return lax.optimization_barrier((x, *others))[0]


def shards(query_states, key_states, value_states, segment_ids, pair_margins, upstream, out_weight):
    d = lax.axis_index("dp")
    t = lax.axis_index("tensor")
    y, low = t // 2, t % 2
    place = jnp.stack([y, low, (d // 2) % 2, d % 2]).astype(jnp.int32)
    query, key, value = query_states[0], key_states[0], value_states[0]
    heads, width = out_weight.shape

    weight = lax.all_gather(out_weight, "dp", axis=0, tiled=True, axis_index_groups=Z_GROUPS).reshape(4, heads, width)
    ids = segment_ids[0]
    partner = named("ids_pair", pair, ids)
    segs = jnp.broadcast_to(ids[:, None], (ids.shape[0], HD))
    own, to_sibling, to_across, to_diagonal = prep(place, pair_margins, segs, upstream[0])

    from_across = named("other_across", across, to_across)
    from_diagonal = named("other_diagonal", diagonal, to_diagonal)
    both = jnp.where(low == 0, jnp.stack([ids, partner]), jnp.stack([partner, ids]))
    next_ids = named("ids_next", lambda x: lax.ppermute(x, "tensor", by_tensor(lambda i: i ^ 2)), both)
    half = jnp.where(y % 2 == 0, jnp.stack([both, next_ids]), jnp.stack([next_ids, both]))
    rest_ids = named("ids_rest", lambda x: lax.ppermute(x, "tensor", by_tensor(lambda i: i ^ 4)), half)
    ids = jnp.where(y < 2, jnp.stack([half, rest_ids]), jnp.stack([rest_ids, half])).reshape(-1)
    whole_segs = jnp.broadcast_to(ids[:, None], (ids.shape[0], HD))

    from_sibling = named("near_sibling", sibling, after(to_sibling, partner))
    near = jnp.stack([own, after(from_sibling, rest_ids)])
    n_up, n_down = named("n_up", y_up, near), named("n_down", y_down, near)
    attn_out, stats, bias = forward(place, whole_segs, query, key, value)
    other = jnp.stack([after(from_across, n_up, n_down, attn_out), from_diagonal])

    n, o = near, other
    n_far, o_down = named("n_far", y_up, n_up), named("o_down", y_down, o)
    f = named("pair", pair, jnp.stack([near, other]))
    out_across = named("out_across", across, after(attn_out, f, n_far, o_down))
    o_up, o_far = named("o_up", y_up, after(o, n_far, o_down)), named("o_far", y_down, o_down)
    f = after(f, o_up, o_far)
    f_up, f_down = named("f_up", y_up, f), named("f_down", y_down, f)
    f_far = [named("f_far_up", y_up, f_up[0]), named("f_far_down", y_down, f_down[1])]
    same = [(x[None], 0) for x in (n, n_down, n_far, n_up, o, o_down, o_far, o_up)]
    flip = [x for p in range(2) for x in ((f, p), (f_down, p), (f_far[p][None], 0), (f_up, p))]

    def sums(name, pieces):
        keep_near, keep_other, give = partial(pieces, weight)
        given = named(name + "_sibling", sibling, give)
        total = (keep_other + given[1].astype(F32)).astype(BF16)
        return keep_near, given, named(name + "_across", across, total)

    terms_same = sums("sum_same", same)
    out_near = named("out_near", sibling, after(attn_out, o_up, o_far))
    out_other = named("out_other", sibling, after(out_across, o_up, o_far))
    outs = (attn_out, out_near, out_across, after(out_other, terms_same[1]))
    total = wgrad(same, flip, outs).reshape(4 * heads, width)
    weight_grad = lax.psum_scatter(after(total, terms_same[2]), "dp", scatter_dimension=0, tiled=True, axis_index_groups=Z_GROUPS)
    terms_flip = sums("sum_flip", [(after(f, total), 0), *flip[1:]])
    dq, dk, dv = backward(place, query, key, value, stats, bias, [*terms_same, *terms_flip])
    return (dq[None], dk[None], dv[None], weight_grad.astype(F32))


def solution(mesh):
    in_specs = (
        P("dp", None, "tensor"),
        P("dp", None, "tensor"),
        P("dp", None, "tensor"),
        P("dp", "tensor"),
        P("dp", None),
        P("dp", "tensor", None),
        P("tensor", "dp"),
    )
    out_specs = (
        P("dp", None, "tensor"),
        P("dp", None, "tensor"),
        P("dp", None, "tensor"),
        P("tensor", "dp"),
    )
    return jax.shard_map(shards, mesh=mesh, in_specs=in_specs, out_specs=out_specs, check_vma=False)
```

```python
import functools

import jax
import jax.numpy as jnp
from jax import lax
from jax.experimental import pallas as pl
from jax.experimental.pallas import tpu as pltpu
from jax.sharding import PartitionSpec as P

HD = 128
F32 = jnp.float32
BF16 = jnp.bfloat16
SCALE = HD ** (-0.5)
VMEM_MOST = 60 * 1024 * 1024


def by_dp(step):
    return [(i, step(i)) for i in range(16)]


def by_tensor(step):
    return [(i, step(i)) for i in range(8)]


SIBLING = by_dp(lambda i: i ^ 1)
ACROSS = by_dp(lambda i: i ^ 2)
DIAGONAL = by_dp(lambda i: i ^ 3)
PAIR = by_tensor(lambda i: i ^ 1)
Y_UP = by_tensor(lambda i: (i + 2) % 8)
Y_DOWN = by_tensor(lambda i: (i - 2) % 8)
Z_UP = by_dp(lambda i: (i + 4) % 16)
Z_DOWN = by_dp(lambda i: (i - 4) % 16)
Z_GROUPS = [[z * 4 + j for z in range(4)] for j in range(4)]


def sibling(x):
    return lax.ppermute(x, "dp", SIBLING)


def across(x):
    return lax.ppermute(x, "dp", ACROSS)


def diagonal(x):
    return lax.ppermute(x, "dp", DIAGONAL)


def pair(x):
    return lax.ppermute(x, "tensor", PAIR)


def z_up(x):
    return lax.ppermute(x, "dp", Z_UP)


def z_down(x):
    return lax.ppermute(x, "dp", Z_DOWN)


def y_up(x):
    return lax.ppermute(x, "tensor", Y_UP)


def y_down(x):
    return lax.ppermute(x, "tensor", Y_DOWN)


def nn(a, b):
    return lax.dot_general(a, b, (((1,), (0,)), ((), ())), preferred_element_type=F32)


def nt(a, b):
    return lax.dot_general(a, b, (((1,), (1,)), ((), ())), preferred_element_type=F32)


def cost(us):
    return pl.CostEstimate(flops=0, bytes_accessed=int(us * 3e6), transcendentals=0)


def params():
    return pltpu.CompilerParams(vmem_limit_bytes=VMEM_MOST, dimension_semantics=("arbitrary",))


SMEM = functools.partial(pl.BlockSpec, memory_space=pltpu.SMEM)


def whole(shape):
    return pl.BlockSpec(shape, lambda i: (0,) * len(shape))


def prep_kernel(place, margins, segs, up, own, to_sibling, to_across, to_diagonal):
    h, c = place[2], place[3]
    seg = segs[...]
    margin = jnp.full(seg.shape, margins[0, 0], F32)
    for p in range(1, margins.shape[1]):
        margin = jnp.where((seg >> 1) == p, margins[0, p], margin)
    factor = jax.nn.sigmoid(-margin) * jnp.where((seg & 1) == 0, -1.0, 1.0)
    width = own.shape[1]
    factor = jnp.concatenate([factor] * (width // factor.shape[1]), axis=1)

    def grad(hh, cc):
        start = pl.multiple_of((hh * 2 + cc) * width, width)
        return (up[:, pl.ds(start, width)].astype(F32) * factor).astype(BF16)

    own[...] = grad(h, c)
    to_sibling[...] = grad(h, 1 - c)
    to_across[...] = grad(1 - h, c)
    to_diagonal[...] = grad(1 - h, 1 - c)


def prep(place, margins, segs, up):
    seq, model = up.shape
    width = model // 16
    col = pl.BlockSpec((seq, width), lambda i: (0, i))
    return pl.pallas_call(
        prep_kernel,
        grid=(4,),
        in_specs=[SMEM(), SMEM(), whole(segs.shape), pl.BlockSpec((seq, 4 * width), lambda i: (0, i))],
        out_specs=[col] * 4,
        out_shape=[jax.ShapeDtypeStruct((seq, 4 * width), BF16)] * 4,
        compiler_params=params(),
        cost_estimate=cost(3),
        name="prep",
    )(place, margins, segs, up)


def key_range(block):
    return max(0, block - 2) * HD, (block + 1) * HD


def two_heads(ref, block):
    rows = slice(block * HD, (block + 1) * HD)
    return jnp.concatenate([ref[rows, :HD], ref[rows, HD:]], axis=0)


def twice(x):
    return jnp.concatenate([x, x], axis=1)


def forward_kernel(place, segs, q, k, v, out, stats, bias, v_t):
    y, low = place[0], place[1]
    blocks = q.shape[0] // HD

    @pl.when(pl.program_id(0) == 0)
    def _():
        v_t[...] = v[...].astype(F32).T.astype(BF16)
        for b in range(blocks):
            first, last = key_range(b)
            of_query = segs[b * HD : (b + 1) * HD, :].astype(F32).T[:1]
            of_key = segs[first:last, :].astype(F32)
            shape = (last - first, HD)
            query_at = lax.broadcasted_iota(jnp.int32, shape, 1) + b * HD
            key_at = lax.broadcasted_iota(jnp.int32, shape, 0) + first
            seen = (of_key == of_query) & (key_at <= query_at)
            bias[b, : last - first] = jnp.where(seen, 0.0, -1e30)

    for b in range(blocks):
        first, last = key_range(b)
        q2 = two_heads(q, b)
        s = nt(k[first:last], q2) * SCALE + twice(bias[b, : last - first])
        highest = jnp.max(s, axis=0, keepdims=True)
        e = jnp.exp(s - highest)
        inverse = 1.0 / jnp.sum(e, axis=0, keepdims=True)
        stats[0, b : b + 1] = highest
        stats[0, blocks + b : blocks + b + 1] = inverse
        a = nn(v_t[:, first:last], (e * inverse).astype(BF16))
        at = pl.multiple_of(lax.rem(b - y + 4, 4) * HD, HD)
        for i in range(2):
            x = a[:, i * HD : (i + 1) * HD]
            x = jnp.where(low == 0, x, pltpu.roll(x, HD // 2, 1))
            out[i * HD : (i + 1) * HD, pl.ds(at, HD)] = x.astype(BF16)


def forward(place, segs, q, k, v):
    length, wide = q.shape
    pairs, blocks = wide // (2 * HD), length // HD
    bias_shape = (blocks, 3 * HD, HD)
    return pl.pallas_call(
        forward_kernel,
        grid=(pairs,),
        in_specs=[
            SMEM(),
            whole(segs.shape),
            pl.BlockSpec((length, 2 * HD), lambda i: (0, i)),
            whole(k.shape),
            whole(v.shape),
        ],
        out_specs=[
            pl.BlockSpec((2 * HD, length), lambda i: (i, 0)),
            pl.BlockSpec((1, 2 * blocks, 2 * HD), lambda i: (i, 0, 0)),
            whole(bias_shape),
        ],
        out_shape=[
            jax.ShapeDtypeStruct((wide, length), BF16),
            jax.ShapeDtypeStruct((pairs, 2 * blocks, 2 * HD), F32),
            jax.ShapeDtypeStruct(bias_shape, F32),
        ],
        scratch_shapes=[pltpu.VMEM((HD, length), BF16)],
        compiler_params=params(),
        cost_estimate=cost(9),
        name="attend",
    )(place, segs, q, k, v)


def backward_kernel(place, q, k, v, stats, bias, *rest):
    terms, (dq, dk, dv, k_t, dk_sum, dv_sum) = rest[:6], rest[6:]
    y, low = place[0], place[1]
    blocks = q.shape[0] // HD
    half = HD // 2

    @pl.when(pl.program_id(0) == 0)
    def _():
        k_t[...] = k[...].astype(F32).T.astype(BF16)
        dk_sum[...] = jnp.zeros_like(dk_sum)
        dv_sum[...] = jnp.zeros_like(dv_sum)

    for b in range(blocks):
        first, last = key_range(b)
        at = lax.rem(b - y + 4, 4)

        def term(first, k):
            rows = pl.ds(pl.multiple_of(k * half, half), half)
            return terms[first][rows] + terms[first + 1][rows].astype(F32) + terms[first + 2][rows].astype(F32)

        same = term(0, at)
        flip = term(3, at)
        grad = jnp.concatenate([jnp.where(low == 0, same, flip), jnp.where(low == 0, flip, same)], axis=0).astype(BF16)
        grad = jnp.concatenate([grad[:, :HD], grad[:, HD:]], axis=0)
        q2 = two_heads(q, b)
        s = nt(k[first:last], q2) * SCALE + twice(bias[b, : last - first])
        p = jnp.exp(s - stats[0, b : b + 1]) * stats[0, blocks + b : blocks + b + 1]
        dp = nt(v[first:last], grad)
        delta = jnp.sum(p * dp, axis=0, keepdims=True)
        ds = (SCALE * p * (dp - delta)).astype(BF16)
        dv_sum[first:last] += nn(p.astype(BF16), grad)
        dk_sum[first:last] += nn(ds, q2)
        x = nn(k_t[:, first:last], ds)
        for i in range(2):
            dq[b * HD : (b + 1) * HD, i * HD : (i + 1) * HD] = x[:, i * HD : (i + 1) * HD].T.astype(BF16)

    @pl.when(pl.program_id(0) == pl.num_programs(0) - 1)
    def _():
        dk[...] = dk_sum[...].astype(BF16)
        dv[...] = dv_sum[...].astype(BF16)


def backward(place, q, k, v, stats, bias, terms):
    length, wide = q.shape
    pairs, blocks = wide // (2 * HD), length // HD
    two = pl.BlockSpec((length, 2 * HD), lambda i: (0, i))
    return pl.pallas_call(
        backward_kernel,
        grid=(pairs,),
        in_specs=[
            SMEM(),
            two,
            whole(k.shape),
            whole(v.shape),
            pl.BlockSpec((1, 2 * blocks, 2 * HD), lambda i: (i, 0, 0)),
            whole(bias.shape),
        ]
        + [pl.BlockSpec((x.shape[0], 2 * HD), lambda i: (0, i)) for x in terms],
        out_specs=[two, whole(k.shape), whole(v.shape)],
        out_shape=[jax.ShapeDtypeStruct(x.shape, BF16) for x in (q, k, v)],
        scratch_shapes=[pltpu.VMEM((HD, length), BF16), pltpu.VMEM(k.shape, F32), pltpu.VMEM(v.shape, F32)],
        compiler_params=params(),
        cost_estimate=cost(9),
        name="attend_grad",
    )(place, q, k, v, stats, bias, *terms)


def partial_kernel(count, *refs):
    pieces, (weight, keep_near, keep_other, give_near, give_other, x) = refs[:-6], refs[-6:]
    seq = pieces[0].shape[2]
    half = count * seq

    @pl.when(pl.program_id(0) == 0)
    def _():
        for p in range(2):
            for i in range(2):
                for k in range(count):
                    at = (p * 2 + i) * half + k * seq
                    x[at : at + seq] = pieces[p * count + k][0, i]

    w = jnp.concatenate([weight[j] for j in range(4)], axis=1)
    for p, (keep, give) in enumerate(((keep_near, give_near), (keep_other, give_other))):
        total = nt(x[p * 2 * half : (p + 1) * 2 * half], w)
        keep[...] = total[:half]
        give[...] = total[half:].astype(BF16)


def partial(pieces, weight, us):
    _, _, seq, cols = pieces[0][0].shape
    heads = weight.shape[1]
    tile = heads // 2
    count = len(pieces) // 2
    rows = count * seq
    out = pl.BlockSpec((rows, tile), lambda i: (0, i))

    def spec(index):
        return pl.BlockSpec((1, 2, seq, cols), lambda i: (index, 0, 0, 0))

    return pl.pallas_call(
        functools.partial(partial_kernel, count),
        grid=(2,),
        in_specs=[spec(index) for _, index in pieces] + [pl.BlockSpec((4, tile, cols // 4), lambda i: (0, i, 0))],
        out_specs=[out] * 4,
        out_shape=[jax.ShapeDtypeStruct((rows, heads), dtype) for dtype in (F32, F32, BF16, BF16)],
        scratch_shapes=[pltpu.VMEM((4 * rows, cols), BF16)],
        compiler_params=params(),
        cost_estimate=cost(us),
        name="partial_grad",
    )(*[x for x, _ in pieces], weight)


def wgrad_kernel(place, *refs):
    same, flip, outs, results, x = refs[:8], refs[8:16], refs[16:20], refs[20:25], refs[25]
    seq = same[0].shape[2]
    length = 8 * seq
    for p in range(2):
        for i in range(2):
            for k in range(4):
                at = (p * 2 + i) * length + 2 * k * seq
                x[at : at + seq] = same[p * 4 + k][0, i]
                x[at + seq : at + 2 * seq] = flip[p * 4 + k][0, i]
    up, down, ahead, behind, mine = results
    rows = ahead.shape[0]
    places = ((up.at[0], down.at[0]), (ahead, up.at[1]), (down.at[1], behind), (mine.at[:rows], mine.at[rows:]))
    tile = 256
    for m in range(0, 2 * rows, tile):
        total = nn(outs[0][m : m + tile], x[:length])
        for r in range(1, 4):
            total += nn(outs[r][m : m + tile], x[r * length : (r + 1) * length])
        total = total.astype(BF16)
        for step, halves in enumerate(places):

            @pl.when(pl.program_id(0) == step)
            def _():
                halves[m // rows][m % rows : m % rows + tile] = total


def wgrad(place, same, flip, outs):
    _, _, seq, cols = same[0][0].shape
    heads = outs[0].shape[0]
    width = cols // 4

    def spec(index):
        def at(i, place):
            return index, 0, 0, lax.rem(place[4] + jnp.where(i == 0, 2, jnp.where(i == 1, 1, jnp.where(i == 2, 3, 0))), 4)

        return pl.BlockSpec((1, 2, seq, width), at)

    half = (heads // 2, width)
    results = [(2, *half), (2, *half), half, half, (heads, width)]
    return pl.pallas_call(
        wgrad_kernel,
        grid_spec=pltpu.PrefetchScalarGridSpec(
            num_scalar_prefetch=1,
            grid=(4,),
            in_specs=[spec(index) for _, index in same + flip] + [pl.BlockSpec(outs[0].shape, lambda i, place: (0, 0))] * 4,
            out_specs=[pl.BlockSpec(r, lambda i, place, n=len(r): (0,) * n) for r in results],
            scratch_shapes=[pltpu.VMEM((32 * seq, width), BF16)],
        ),
        out_shape=[jax.ShapeDtypeStruct(r, BF16) for r in results],
        compiler_params=params(),
        cost_estimate=cost(14),
        name="weight_grad",
    )(place, *[x for x, _ in same + flip], *outs)


def named(name, fn, x):
    with jax.named_scope("t_" + name):
        return fn(x)


def after(x, *others):
    return lax.optimization_barrier((x, *others))[0]


def shards(query_states, key_states, value_states, segment_ids, pair_margins, upstream, out_weight):
    d = lax.axis_index("dp")
    t = lax.axis_index("tensor")
    y, low = t // 2, t % 2
    place = jnp.stack([y, low, (d // 2) % 2, d % 2, d // 4]).astype(jnp.int32)
    query, key, value = query_states[0], key_states[0], value_states[0]
    heads, width = out_weight.shape

    weight = lax.all_gather(out_weight, "dp", axis=0, tiled=True, axis_index_groups=Z_GROUPS).reshape(4, heads, width)
    ids = segment_ids[0]
    partner = named("ids_pair", pair, ids)
    segs = jnp.broadcast_to(ids[:, None], (ids.shape[0], HD))
    own, to_sibling, to_across, to_diagonal = prep(place, pair_margins, segs, upstream[0])

    from_across = named("other_across", across, to_across)
    from_diagonal = named("other_diagonal", diagonal, to_diagonal)
    both = jnp.where(low == 0, jnp.stack([ids, partner]), jnp.stack([partner, ids]))
    next_ids = named("ids_next", lambda x: lax.ppermute(x, "tensor", by_tensor(lambda i: i ^ 2)), both)
    half = jnp.where(y % 2 == 0, jnp.stack([both, next_ids]), jnp.stack([next_ids, both]))
    rest_ids = named("ids_rest", lambda x: lax.ppermute(x, "tensor", by_tensor(lambda i: i ^ 4)), half)
    ids = jnp.where(y < 2, jnp.stack([half, rest_ids]), jnp.stack([rest_ids, half])).reshape(-1)
    whole_segs = jnp.broadcast_to(ids[:, None], (ids.shape[0], HD))

    from_sibling = named("near_sibling", sibling, after(to_sibling, partner))
    near = jnp.stack([own, after(from_sibling, rest_ids)])
    n_up, n_down = named("n_up", y_up, near), named("n_down", y_down, near)
    attn_out, stats, bias = forward(place, whole_segs, query, key, value)
    other = jnp.stack([after(from_across, n_up, n_down, attn_out), from_diagonal])

    n, o = near, other
    n_far, o_down = named("n_far", y_up, n_up), named("o_down", y_down, o)
    f = named("pair", pair, jnp.stack([near, other]))
    out_across = named("out_across", across, after(attn_out, f, n_far, o_down))
    o_up, o_far = named("o_up", y_up, after(o, n_far, o_down)), named("o_far", y_down, o_down)
    f = after(f, o_up, o_far)
    f_up, f_down = named("f_up", y_up, f), named("f_down", y_down, f)
    same = [(x[None], 0) for x in (n, n_down, n_far, n_up, o, o_down, o_far, o_up)]
    def sums(name, pieces, us):
        keep_near, keep_other, give_near, give_other = partial(pieces, weight, us)
        given = named(name + "_sibling", sibling, give_other)
        total = (keep_other + given.astype(F32)).astype(BF16)
        return keep_near, give_near, given, named(name + "_across", across, total)

    same_near, give_same, got_same, sent_same = sums("sum_same", same, 9)
    f_far = [named("f_far_up", y_up, after(f_up, same_near)[0]), named("f_far_down", y_down, f_down[1])]
    flip = [x for p in range(2) for x in ((f, p), (f_down, p), (f_far[p][None], 0), (f_up, p))]
    out_near = named("out_near", sibling, after(attn_out, same_near))
    out_other = named("out_other", sibling, after(out_across, same_near))
    outs = (attn_out, out_near, out_across, after(out_other, got_same))

    up, down, ahead, behind, mine = wgrad(place, same, flip, outs)
    from_below, from_above = named("wg_up", z_up, after(up, sent_same)), named("wg_down", z_down, after(down, sent_same))

    def add(*xs):
        return sum(x.astype(F32) for x in xs)

    given_same = named("same_near", sibling, after(give_same, mine))
    flip_near, give_flip, got_flip, sent_flip = sums("sum_flip", [(after(f, given_same), 0), *flip[1:]], 1)
    given_flip = named("flip_near", sibling, give_flip)
    from_below, from_above, _ = lax.optimization_barrier((from_below, from_above, got_flip))
    ahead_sum = named("wg_ahead", z_up, add(ahead, from_below[0]).astype(BF16))
    behind_sum = named("wg_behind", z_down, add(behind, from_above[0]).astype(BF16))
    terms = [same_near, given_same, sent_same, flip_near, given_flip, sent_flip]
    dq, dk, dv = backward(place, query, key, value, stats, bias, terms)
    ahead_sum = after(ahead_sum, dq)
    weight_grad = add(mine, jnp.concatenate([ahead_sum, from_below[1]]), jnp.concatenate([from_above[1], behind_sum]))
    return (dq[None], dk[None], dv[None], weight_grad)


def solution(mesh):
    in_specs = (
        P("dp", None, "tensor"),
        P("dp", None, "tensor"),
        P("dp", None, "tensor"),
        P("dp", "tensor"),
        P("dp", None),
        P("dp", "tensor", None),
        P("tensor", "dp"),
    )
    out_specs = (
        P("dp", None, "tensor"),
        P("dp", None, "tensor"),
        P("dp", None, "tensor"),
        P("tensor", "dp"),
    )
    return jax.shard_map(shards, mesh=mesh, in_specs=in_specs, out_specs=out_specs, check_vma=False)
```

```python
import functools

import jax
import jax.numpy as jnp
from jax import lax
from jax.experimental import pallas as pl
from jax.experimental.pallas import tpu as pltpu
from jax.sharding import PartitionSpec as P

HD = 128
F32 = jnp.float32
BF16 = jnp.bfloat16
SCALE = HD ** (-0.5)
VMEM_MOST = 60 * 1024 * 1024


def by_dp(step):
    return [(i, step(i)) for i in range(16)]


def by_tensor(step):
    return [(i, step(i)) for i in range(8)]


SIBLING = by_dp(lambda i: i ^ 1)
ACROSS = by_dp(lambda i: i ^ 2)
DIAGONAL = by_dp(lambda i: i ^ 3)
PAIR = by_tensor(lambda i: i ^ 1)
Y_UP = by_tensor(lambda i: (i + 2) % 8)
Y_DOWN = by_tensor(lambda i: (i - 2) % 8)
Z_UP = by_dp(lambda i: (i + 4) % 16)
Z_DOWN = by_dp(lambda i: (i - 4) % 16)
Z_GROUPS = [[z * 4 + j for z in range(4)] for j in range(4)]


def sibling(x):
    return lax.ppermute(x, "dp", SIBLING)


def across(x):
    return lax.ppermute(x, "dp", ACROSS)


def diagonal(x):
    return lax.ppermute(x, "dp", DIAGONAL)


def pair(x):
    return lax.ppermute(x, "tensor", PAIR)


def z_up(x):
    return lax.ppermute(x, "dp", Z_UP)


def z_down(x):
    return lax.ppermute(x, "dp", Z_DOWN)


def y_up(x):
    return lax.ppermute(x, "tensor", Y_UP)


def y_down(x):
    return lax.ppermute(x, "tensor", Y_DOWN)


def nn(a, b):
    return lax.dot_general(a, b, (((1,), (0,)), ((), ())), preferred_element_type=F32)


def nt(a, b):
    return lax.dot_general(a, b, (((1,), (1,)), ((), ())), preferred_element_type=F32)


def cost(us):
    return pl.CostEstimate(flops=0, bytes_accessed=int(us * 3e6), transcendentals=0)


def params():
    return pltpu.CompilerParams(vmem_limit_bytes=VMEM_MOST, dimension_semantics=("arbitrary",))


SMEM = functools.partial(pl.BlockSpec, memory_space=pltpu.SMEM)


def whole(shape):
    return pl.BlockSpec(shape, lambda i: (0,) * len(shape))


def prep_kernel(place, margins, segs, up, own, to_sibling, to_across, to_diagonal):
    h, c = place[2], place[3]
    seg = segs[...]
    margin = jnp.full(seg.shape, margins[0, 0], F32)
    for p in range(1, margins.shape[1]):
        margin = jnp.where((seg >> 1) == p, margins[0, p], margin)
    factor = jax.nn.sigmoid(-margin) * jnp.where((seg & 1) == 0, -1.0, 1.0)
    width = own.shape[1]
    factor = jnp.concatenate([factor] * (width // factor.shape[1]), axis=1)

    def grad(hh, cc):
        start = pl.multiple_of((hh * 2 + cc) * width, width)
        return (up[:, pl.ds(start, width)].astype(F32) * factor).astype(BF16)

    own[...] = grad(h, c)
    to_sibling[...] = grad(h, 1 - c)
    to_across[...] = grad(1 - h, c)
    to_diagonal[...] = grad(1 - h, 1 - c)


def prep(place, margins, segs, up):
    seq, model = up.shape
    width = model // 16
    col = pl.BlockSpec((seq, width), lambda i: (0, i))
    return pl.pallas_call(
        prep_kernel,
        grid=(4,),
        in_specs=[SMEM(), SMEM(), whole(segs.shape), pl.BlockSpec((seq, 4 * width), lambda i: (0, i))],
        out_specs=[col] * 4,
        out_shape=[jax.ShapeDtypeStruct((seq, 4 * width), BF16)] * 4,
        compiler_params=params(),
        cost_estimate=cost(3),
        name="prep",
    )(place, margins, segs, up)


def key_range(block):
    return max(0, block - 2) * HD, (block + 1) * HD


def two_heads(ref, block):
    rows = slice(block * HD, (block + 1) * HD)
    return jnp.concatenate([ref[rows, :HD], ref[rows, HD:]], axis=0)


def twice(x):
    return jnp.concatenate([x, x], axis=1)


def forward_kernel(place, segs, q, k, v, out, stats, bias, v_t):
    y, low = place[0], place[1]
    blocks = q.shape[0] // HD

    @pl.when(pl.program_id(0) == 0)
    def _():
        v_t[...] = v[...].astype(F32).T.astype(BF16)
        for b in range(blocks):
            first, last = key_range(b)
            of_query = segs[b * HD : (b + 1) * HD, :].astype(F32).T[:1]
            of_key = segs[first:last, :].astype(F32)
            shape = (last - first, HD)
            query_at = lax.broadcasted_iota(jnp.int32, shape, 1) + b * HD
            key_at = lax.broadcasted_iota(jnp.int32, shape, 0) + first
            seen = (of_key == of_query) & (key_at <= query_at)
            bias[b, : last - first] = jnp.where(seen, 0.0, -1e30)

    for b in range(blocks):
        first, last = key_range(b)
        q2 = two_heads(q, b)
        s = nt(k[first:last], q2) * SCALE + twice(bias[b, : last - first])
        highest = jnp.max(s, axis=0, keepdims=True)
        e = jnp.exp(s - highest)
        inverse = 1.0 / jnp.sum(e, axis=0, keepdims=True)
        stats[0, b : b + 1] = highest
        stats[0, blocks + b : blocks + b + 1] = inverse
        a = nn(v_t[:, first:last], (e * inverse).astype(BF16))
        at = pl.multiple_of(lax.rem(b - y + 4, 4) * HD, HD)
        for i in range(2):
            x = a[:, i * HD : (i + 1) * HD]
            x = jnp.where(low == 0, x, pltpu.roll(x, HD // 2, 1))
            out[i * HD : (i + 1) * HD, pl.ds(at, HD)] = x.astype(BF16)


def forward(place, segs, q, k, v):
    length, wide = q.shape
    pairs, blocks = wide // (2 * HD), length // HD
    bias_shape = (blocks, 3 * HD, HD)
    return pl.pallas_call(
        forward_kernel,
        grid=(pairs,),
        in_specs=[
            SMEM(),
            whole(segs.shape),
            pl.BlockSpec((length, 2 * HD), lambda i: (0, i)),
            whole(k.shape),
            whole(v.shape),
        ],
        out_specs=[
            pl.BlockSpec((2 * HD, length), lambda i: (i, 0)),
            pl.BlockSpec((1, 2 * blocks, 2 * HD), lambda i: (i, 0, 0)),
            whole(bias_shape),
        ],
        out_shape=[
            jax.ShapeDtypeStruct((wide, length), BF16),
            jax.ShapeDtypeStruct((pairs, 2 * blocks, 2 * HD), F32),
            jax.ShapeDtypeStruct(bias_shape, F32),
        ],
        scratch_shapes=[pltpu.VMEM((HD, length), BF16)],
        compiler_params=params(),
        cost_estimate=cost(9),
        name="attend",
    )(place, segs, q, k, v)


def backward_kernel(place, q, k, v, stats, bias, *rest):
    terms, (dq, dk, dv, k_t, dk_sum, dv_sum) = rest[:6], rest[6:]
    y, low = place[0], place[1]
    blocks = q.shape[0] // HD
    half = HD // 2

    @pl.when(pl.program_id(0) == 0)
    def _():
        k_t[...] = k[...].astype(F32).T.astype(BF16)
        dk_sum[...] = jnp.zeros_like(dk_sum)
        dv_sum[...] = jnp.zeros_like(dv_sum)

    for b in range(blocks):
        first, last = key_range(b)
        at = lax.rem(b - y + 4, 4)

        def term(first, k):
            rows = pl.ds(pl.multiple_of(k * half, half), half)
            return terms[first][rows] + terms[first + 1][rows].astype(F32) + terms[first + 2][rows].astype(F32)

        same = term(0, at)
        flip = term(3, at)
        grad = jnp.concatenate([jnp.where(low == 0, same, flip), jnp.where(low == 0, flip, same)], axis=0).astype(BF16)
        grad = jnp.concatenate([grad[:, :HD], grad[:, HD:]], axis=0)
        q2 = two_heads(q, b)
        s = nt(k[first:last], q2) * SCALE + twice(bias[b, : last - first])
        p = jnp.exp(s - stats[0, b : b + 1]) * stats[0, blocks + b : blocks + b + 1]
        dp = nt(v[first:last], grad)
        delta = jnp.sum(p * dp, axis=0, keepdims=True)
        ds = (SCALE * p * (dp - delta)).astype(BF16)
        dv_sum[first:last] += nn(p.astype(BF16), grad)
        dk_sum[first:last] += nn(ds, q2)
        x = nn(k_t[:, first:last], ds)
        for i in range(2):
            dq[b * HD : (b + 1) * HD, i * HD : (i + 1) * HD] = x[:, i * HD : (i + 1) * HD].T.astype(BF16)

    @pl.when(pl.program_id(0) == pl.num_programs(0) - 1)
    def _():
        dk[...] = dk_sum[...].astype(BF16)
        dv[...] = dv_sum[...].astype(BF16)


def backward(place, q, k, v, stats, bias, terms):
    length, wide = q.shape
    pairs, blocks = wide // (2 * HD), length // HD
    two = pl.BlockSpec((length, 2 * HD), lambda i: (0, i))
    return pl.pallas_call(
        backward_kernel,
        grid=(pairs,),
        in_specs=[
            SMEM(),
            two,
            whole(k.shape),
            whole(v.shape),
            pl.BlockSpec((1, 2 * blocks, 2 * HD), lambda i: (i, 0, 0)),
            whole(bias.shape),
        ]
        + [pl.BlockSpec((x.shape[0], 2 * HD), lambda i: (0, i)) for x in terms],
        out_specs=[two, whole(k.shape), whole(v.shape)],
        out_shape=[jax.ShapeDtypeStruct(x.shape, BF16) for x in (q, k, v)],
        scratch_shapes=[pltpu.VMEM((HD, length), BF16), pltpu.VMEM(k.shape, F32), pltpu.VMEM(v.shape, F32)],
        compiler_params=params(),
        cost_estimate=cost(9),
        name="attend_grad",
    )(place, q, k, v, stats, bias, *terms)


def partial_kernel(count, *refs):
    pieces, (weight, keep_near, keep_other, give_near, give_other, x) = refs[:-6], refs[-6:]
    seq = pieces[0].shape[2]
    half = count * seq

    @pl.when(pl.program_id(0) == 0)
    def _():
        for p in range(2):
            for i in range(2):
                for k in range(count):
                    at = (p * 2 + i) * half + k * seq
                    x[at : at + seq] = pieces[p * count + k][0, i]

    w = jnp.concatenate([weight[j] for j in range(4)], axis=1)
    for p, (keep, give) in enumerate(((keep_near, give_near), (keep_other, give_other))):
        total = nt(x[p * 2 * half : (p + 1) * 2 * half], w)
        keep[...] = total[:half]
        give[...] = total[half:].astype(BF16)


def partial(pieces, weight, us):
    _, _, seq, cols = pieces[0][0].shape
    heads = weight.shape[1]
    tile = heads // 2
    count = len(pieces) // 2
    rows = count * seq
    out = pl.BlockSpec((rows, tile), lambda i: (0, i))

    def spec(index):
        return pl.BlockSpec((1, 2, seq, cols), lambda i: (index, 0, 0, 0))

    return pl.pallas_call(
        functools.partial(partial_kernel, count),
        grid=(2,),
        in_specs=[spec(index) for _, index in pieces] + [pl.BlockSpec((4, tile, cols // 4), lambda i: (0, i, 0))],
        out_specs=[out] * 4,
        out_shape=[jax.ShapeDtypeStruct((rows, heads), dtype) for dtype in (F32, F32, BF16, BF16)],
        scratch_shapes=[pltpu.VMEM((4 * rows, cols), BF16)],
        compiler_params=params(),
        cost_estimate=cost(us),
        name="partial_grad",
    )(*[x for x, _ in pieces], weight)


def wgrad_kernel(place, *refs):
    same, flip, outs, results, (x, block) = refs[:8], refs[8:16], refs[16:20], refs[20:25], refs[25:]
    seq = same[0].shape[2]
    length = 8 * seq
    for p in range(2):
        for i in range(2):
            for k in range(4):
                at = (p * 2 + i) * length + 2 * k * seq
                x[at : at + seq] = same[p * 4 + k][0, i]
                x[at + seq : at + 2 * seq] = flip[p * 4 + k][0, i]
    up, down, ahead, behind, mine = results
    rows = ahead.shape[0]
    places = ((up.at[0], down.at[0]), (ahead, up.at[1]), (down.at[1], behind), (mine.at[:rows], mine.at[rows:]))
    tile = 256
    for m in range(0, 2 * rows, tile):
        total = nn(outs[0][m : m + tile], x[:length])
        for r in range(1, 4):
            total += nn(outs[r][m : m + tile], x[r * length : (r + 1) * length])
        block[m : m + tile] = total.astype(BF16)
    for step, (first, second) in enumerate(places):

        @pl.when(pl.program_id(0) == step)
        def _():
            first[...] = block[:rows]
            second[...] = block[rows:]


def wgrad(place, same, flip, outs):
    _, _, seq, cols = same[0][0].shape
    heads = outs[0].shape[0]
    width = cols // 4

    def spec(index):
        def at(i, place):
            return index, 0, 0, lax.rem(place[4] + jnp.where(i == 0, 2, jnp.where(i == 1, 1, jnp.where(i == 2, 3, 0))), 4)

        return pl.BlockSpec((1, 2, seq, width), at)

    half = (heads // 2, width)
    results = [(2, *half), (2, *half), half, half, (heads, width)]
    return pl.pallas_call(
        wgrad_kernel,
        grid_spec=pltpu.PrefetchScalarGridSpec(
            num_scalar_prefetch=1,
            grid=(4,),
            in_specs=[spec(index) for _, index in same + flip] + [pl.BlockSpec(outs[0].shape, lambda i, place: (0, 0))] * 4,
            out_specs=[pl.BlockSpec(r, lambda i, place, n=len(r): (0,) * n) for r in results],
            scratch_shapes=[pltpu.VMEM((32 * seq, width), BF16), pltpu.VMEM((heads, width), BF16)],
        ),
        out_shape=[jax.ShapeDtypeStruct(r, BF16) for r in results],
        compiler_params=params(),
        cost_estimate=cost(14),
        name="weight_grad",
    )(place, *[x for x, _ in same + flip], *outs)


def named(name, fn, x):
    with jax.named_scope("t_" + name):
        return fn(x)


def after(x, *others):
    return lax.optimization_barrier((x, *others))[0]


def shards(query_states, key_states, value_states, segment_ids, pair_margins, upstream, out_weight):
    d = lax.axis_index("dp")
    t = lax.axis_index("tensor")
    y, low = t // 2, t % 2
    place = jnp.stack([y, low, (d // 2) % 2, d % 2, d // 4]).astype(jnp.int32)
    query, key, value = query_states[0], key_states[0], value_states[0]
    heads, width = out_weight.shape

    weight = lax.all_gather(out_weight, "dp", axis=0, tiled=True, axis_index_groups=Z_GROUPS).reshape(4, heads, width)
    ids = segment_ids[0]
    partner = named("ids_pair", pair, ids)
    segs = jnp.broadcast_to(ids[:, None], (ids.shape[0], HD))
    own, to_sibling, to_across, to_diagonal = prep(place, pair_margins, segs, upstream[0])

    from_across = named("other_across", across, to_across)
    from_diagonal = named("other_diagonal", diagonal, to_diagonal)
    both = jnp.where(low == 0, jnp.stack([ids, partner]), jnp.stack([partner, ids]))
    next_ids = named("ids_next", lambda x: lax.ppermute(x, "tensor", by_tensor(lambda i: i ^ 2)), both)
    half = jnp.where(y % 2 == 0, jnp.stack([both, next_ids]), jnp.stack([next_ids, both]))
    rest_ids = named("ids_rest", lambda x: lax.ppermute(x, "tensor", by_tensor(lambda i: i ^ 4)), half)
    ids = jnp.where(y < 2, jnp.stack([half, rest_ids]), jnp.stack([rest_ids, half])).reshape(-1)
    whole_segs = jnp.broadcast_to(ids[:, None], (ids.shape[0], HD))

    from_sibling = named("near_sibling", sibling, after(to_sibling, partner))
    near = jnp.stack([own, after(from_sibling, rest_ids)])
    n_up, n_down = named("n_up", y_up, near), named("n_down", y_down, near)
    attn_out, stats, bias = forward(place, whole_segs, query, key, value)
    other = jnp.stack([after(from_across, n_up, n_down, attn_out), from_diagonal])

    n, o = near, other
    n_far, o_down = named("n_far", y_up, n_up), named("o_down", y_down, o)
    f = named("pair", pair, jnp.stack([near, other]))
    out_across = named("out_across", across, after(attn_out, f, n_far, o_down))
    o_up, o_far = named("o_up", y_up, after(o, n_far, o_down)), named("o_far", y_down, o_down)
    f = after(f, o_up, o_far)
    f_up, f_down = named("f_up", y_up, f), named("f_down", y_down, f)
    same = [(x[None], 0) for x in (n, n_down, n_far, n_up, o, o_down, o_far, o_up)]
    def sums(name, pieces, us):
        keep_near, keep_other, give_near, give_other = partial(pieces, weight, us)
        given = named(name + "_sibling", sibling, give_other)
        total = (keep_other + given.astype(F32)).astype(BF16)
        return keep_near, give_near, given, named(name + "_across", across, total)

    same_near, give_same, got_same, sent_same = sums("sum_same", same, 9)
    f_far = [named("f_far_up", y_up, after(f_up, same_near)[0]), named("f_far_down", y_down, f_down[1])]
    flip = [x for p in range(2) for x in ((f, p), (f_down, p), (f_far[p][None], 0), (f_up, p))]
    out_near = named("out_near", sibling, after(attn_out, same_near))
    out_other = named("out_other", sibling, after(out_across, same_near))
    outs = (attn_out, out_near, out_across, after(out_other, got_same))

    up, down, ahead, behind, mine = wgrad(place, same, flip, outs)
    from_below, from_above = named("wg_up", z_up, after(up, sent_same)), named("wg_down", z_down, after(down, sent_same))

    def add(*xs):
        return sum(x.astype(F32) for x in xs)

    given_same = named("same_near", sibling, after(give_same, mine))
    flip_near, give_flip, got_flip, sent_flip = sums("sum_flip", [(after(f, given_same), 0), *flip[1:]], 1)
    given_flip = named("flip_near", sibling, give_flip)
    from_below, from_above, _ = lax.optimization_barrier((from_below, from_above, got_flip))
    ahead_sum = named("wg_ahead", z_up, add(ahead, from_below[0]).astype(BF16))
    behind_sum = named("wg_behind", z_down, add(behind, from_above[0]).astype(BF16))
    terms = [same_near, given_same, sent_same, flip_near, given_flip, sent_flip]
    dq, dk, dv = backward(place, query, key, value, stats, bias, terms)
    ahead_sum = after(ahead_sum, dq)
    weight_grad = add(mine, jnp.concatenate([ahead_sum, from_below[1]]), jnp.concatenate([from_above[1], behind_sum]))
    return (dq[None], dk[None], dv[None], weight_grad)


def solution(mesh):
    in_specs = (
        P("dp", None, "tensor"),
        P("dp", None, "tensor"),
        P("dp", None, "tensor"),
        P("dp", "tensor"),
        P("dp", None),
        P("dp", "tensor", None),
        P("tensor", "dp"),
    )
    out_specs = (
        P("dp", None, "tensor"),
        P("dp", None, "tensor"),
        P("dp", None, "tensor"),
        P("tensor", "dp"),
    )
    return jax.shard_map(shards, mesh=mesh, in_specs=in_specs, out_specs=out_specs, check_vma=False)
```
